256 devices in a mesh: seq: 64 (over z, y, core), head: 4 (over x).
Axes of the slice: x: 4, y: 4, z: 8, core: 2. Of those that a mesh axis runs over, the one named last changes fastest.
Arguments:
- q_in: bfloat16 [8192, 2048], P('seq', 'head'), may hold values from -6 to 6
- k_in: bfloat16 [8192, 2048], P('seq', 'head'), may hold values from -6 to 6
- v_in: bfloat16 [8192, 4096], P('seq', 'head'), may hold values from -6 to 6
- z_gate: bfloat16 [8192, 4096], P('seq', 'head'), may hold values from -6 to 6
- decay: float32 [8192, 32], P('seq', 'head'), may hold values from -1.5 to 0, as said below
- rate: float32 [8192, 32], P('seq', 'head'), may hold values from 0 to 0.95, as said below
- conv_q: float32 [4, 2048], P(None, 'head'), may hold values from -3 to 3
- conv_k: float32 [4, 2048], P(None, 'head'), may hold values from -3 to 3
- conv_v: float32 [4, 4096], P(None, 'head'), may hold values from -3 to 3
- norm_gain: float32 [128], replicated, may hold values from 0.5 to 1.5
- w_out: bfloat16 [4096, 2048], P('head'), may hold values from -0.09375 to 0.09375
Outputs:
- mixed: bfloat16 [8192, 2048], P('seq', 'head')
The draws below stay inside these ranges and needn't reach their ends.
Inputs may be any that keep to these rules, and one draw needn't show every extreme that they name: `decay`: every entry is negative. `rate`: every entry is positive.
All inputs are finite; a program needn't handle non-finite values.
Results may differ from the reference program's by a relative error of at most 0.0049.
Values may be sent and summed in bfloat16 or wider, within the bound.
A program may use at most 192 MiB of HBM per device.

```python
import jax
import jax.numpy as jnp
from jax import lax

D_MODEL = 2048
KEY_HEADS = 16
VAL_HEADS = 32
HEAD_DIM = 128
GROUP = 64
TOK_DEV = 128
TOKENS = 8192


def gate_layout(key):
    base = jax.random.fold_in(key, 7)
    keys = jax.random.split(base, 5)
    slow_count = VAL_HEADS // 2
    middle_count = VAL_HEADS // 4
    ranking = jax.random.permutation(keys[0], VAL_HEADS)
    gradual_path = (ranking < slow_count).astype(jnp.float32)
    middle_path = jnp.logical_and(ranking >= slow_count, ranking < slow_count + middle_count).astype(jnp.float32)
    per_block = jax.random.uniform(keys[1], (TOKENS // GROUP, 1, VAL_HEADS), minval=0.5, maxval=2.0)
    per_token = jax.random.uniform(keys[2], (TOKENS // GROUP, GROUP, VAL_HEADS), minval=0.5, maxval=1.5)
    coarse_estimate = (per_block * per_token).reshape(TOKENS, VAL_HEADS)
    spots = jax.random.randint(keys[3], (6,), 0, TOKENS)
    level_count = jax.random.uniform(keys[4], (6,), minval=0.22, maxval=0.69)
    match_found = (jnp.arange(TOKENS)[:, None] == spots[None, :]).astype(jnp.float32)
    spike_amount = jnp.sum(match_found * level_count[None, :], axis=1)
    return (gradual_path, middle_path, coarse_estimate, spike_amount)


def draw_decay(key, part):
    gradual_path, middle_path, coarse_estimate, spike_amount = gate_layout(key)
    lasting = gradual_path + middle_path
    gradual_portion = lasting * (-0.5 / TOKENS) * coarse_estimate
    quick_portion = (1.0 - lasting) * (-coarse_estimate / 40.0)
    return (gradual_portion + quick_portion - spike_amount[:, None]).astype(jnp.float32)


def draw_rate(key, part):
    gradual_path, middle_path, coarse_estimate, spike_amount = gate_layout(key)
    quick_path = 1.0 - gradual_path - middle_path
    gradual_portion = gradual_path * (0.4 * HEAD_DIM / TOKENS) * coarse_estimate
    middle_portion = middle_path * (0.25 * HEAD_DIM / TOK_DEV) * coarse_estimate
    quick_portion = quick_path * 0.3 * coarse_estimate
    return (gradual_portion + middle_portion + quick_portion).astype(jnp.float32)


def steps_of(rng, dims, cuts, smallest, high):
    loudness = 1.0
    for dim, shards_of in cuts:
        heights = jax.random.uniform(jax.random.fold_in(jax.random.fold_in(rng, 6), dim), (shards_of,), jnp.float32, smallest / len(cuts), high / len(cuts))
        loudness = loudness * jnp.repeat(jnp.exp(heights), dims[dim] // shards_of).reshape((-1,) + (1,) * (len(dims) - 1 - dim))
    return loudness


def normal_values(own_key, shape, scale, bound, cuts=(), held_as=jnp.bfloat16):
    entries = scale * jax.random.normal(own_key, shape, jnp.float32)
    if cuts:
        entries = entries * steps_of(own_key, shape, cuts, -0.22, 0.18)
    return jnp.clip(entries, -bound, bound).astype(held_as)


def setup_inputs(seed: int = 0) -> dict:
    key_of = jax.random.split(jax.random.key(seed), 12)
    return {
        "q_in": normal_values(key_of[0], (TOKENS, KEY_HEADS * HEAD_DIM), 1.0, 6.0, ((0, 64), (1, 4))),
        "k_in": normal_values(key_of[1], (TOKENS, KEY_HEADS * HEAD_DIM), 1.0, 6.0, ((0, 64), (1, 4))),
        "v_in": normal_values(key_of[2], (TOKENS, VAL_HEADS * HEAD_DIM), 1.0, 6.0, ((0, 64), (1, 4))),
        "z_gate": normal_values(key_of[3], (TOKENS, VAL_HEADS * HEAD_DIM), 1.0, 6.0, ((0, 64), (1, 4))),
        "decay": draw_decay(jax.random.fold_in(key_of[11], 71), 0),
        "rate": draw_rate(jax.random.fold_in(key_of[11], 71), 0),
        "conv_q": normal_values(key_of[6], (4, KEY_HEADS * HEAD_DIM), 4 ** -0.5, 3.0, ((1, 4),), jnp.float32),
        "conv_k": normal_values(key_of[7], (4, KEY_HEADS * HEAD_DIM), 4 ** -0.5, 3.0, ((1, 4),), jnp.float32),
        "conv_v": normal_values(key_of[8], (4, VAL_HEADS * HEAD_DIM), 4 ** -0.5, 3.0, ((1, 4),), jnp.float32),
        "norm_gain": jnp.clip(1.0 + 0.1 * jax.random.normal(key_of[9], (HEAD_DIM,), jnp.float32), 0.5, 1.5),
        "w_out": normal_values(key_of[10], (VAL_HEADS * HEAD_DIM, D_MODEL), (VAL_HEADS * HEAD_DIM) ** -0.5, 0.09375, ((0, 4),)),
    }


def conv_silu(x, taps):
    padded = jnp.pad(x.astype(jnp.float32), ((3, 0), (0, 0)))
    total = taps[0] * padded[0:TOKENS]
    total = total + taps[1] * padded[1:TOKENS + 1]
    total = total + taps[2] * padded[2:TOKENS + 2]
    total = total + taps[3] * padded[3:TOKENS + 3]
    return jax.nn.silu(total)

def reference(q_in, k_in, v_in, z_gate, decay, rate, conv_q, conv_k, conv_v, norm_gain, w_out):
    highest = lax.Precision.HIGHEST
    query = conv_silu(q_in, conv_q).reshape(TOKENS, KEY_HEADS, HEAD_DIM)
    keys = conv_silu(k_in, conv_k).reshape(TOKENS, KEY_HEADS, HEAD_DIM)
    values = conv_silu(v_in, conv_v).reshape(TOKENS, VAL_HEADS, HEAD_DIM)
    query = query * lax.rsqrt(lax.optimization_barrier(jnp.sum(query * query, axis=-1, keepdims=True)) + 1e-06) * HEAD_DIM ** (-0.5)
    keys = keys * lax.rsqrt(lax.optimization_barrier(jnp.sum(keys * keys, axis=-1, keepdims=True)) + 1e-06)
    repeat = VAL_HEADS // KEY_HEADS

    def advance(state, inputs):
        q_row, k_row, v_row, g_row, b_row = inputs
        q_rep = jnp.repeat(q_row, repeat, axis=0)
        k_rep = jnp.repeat(k_row, repeat, axis=0)
        decayed = jnp.exp(g_row)[:, None, None] * state
        recalled = jnp.einsum('hd,hde->he', k_rep, decayed, precision=highest)
        state = decayed + b_row[:, None, None] * k_rep[:, :, None] * (v_row - recalled)[:, None, :]
        return (state, jnp.einsum('hd,hde->he', q_rep, state, precision=highest))
    start = jnp.zeros((VAL_HEADS, HEAD_DIM, HEAD_DIM), jnp.float32)
    _, heads_out = lax.scan(advance, start, (query, keys, values, decay, rate))
    scale = lax.rsqrt(lax.optimization_barrier(jnp.mean(heads_out * heads_out, axis=-1, keepdims=True)) + 1e-06)
    gate = jax.nn.silu(z_gate.astype(jnp.float32).reshape(TOKENS, VAL_HEADS, HEAD_DIM))
    gated = (heads_out * scale * norm_gain * gate).astype(jnp.bfloat16).reshape(TOKENS, VAL_HEADS * HEAD_DIM)
    return jnp.dot(gated, w_out, preferred_element_type=jnp.float32).astype(jnp.bfloat16)
```

```python
import jax
import jax.numpy as jnp
from jax import lax
from jax.experimental import pallas as pl
from jax.experimental.pallas import tpu as pltpu
from jax.sharding import PartitionSpec as P

F32 = jnp.float32
BF16 = jnp.bfloat16
D = 128
PLANE = 8
PLANES = 8
HEADS_X = 4
MESH = pl.DeviceIdType.MESH
VMEM = pltpu.VMEM


def split(x):
    high = x.astype(BF16)
    return high, (x - high.astype(F32)).astype(BF16)


def left(x):
    high, low = split(x)
    return jnp.concatenate([high, low], axis=1)


def right(x):
    high, low = split(x)
    both = jnp.concatenate([high, low], axis=1)
    return jnp.concatenate([both, both], axis=0)


def product(lhs, rhs):
    both = jnp.dot(lhs, rhs, preferred_element_type=F32)
    half = both.shape[1] // 2
    return both[:, :half] + both[:, half:]


def silu(x):
    return x / (1.0 + jnp.exp(-x))


def iotas():
    return lax.broadcasted_iota(jnp.int32, (D, D), 0), lax.broadcasted_iota(jnp.int32, (D, D), 1)


def chunk_maps(query, keys, values, gates):
    row, col = iotas()
    rates = gates[1:2, :]
    upper = (row <= col).astype(BF16)
    high = gates.astype(BF16)
    rest = gates - high.astype(F32)
    mid = rest.astype(BF16)
    low = (rest - mid.astype(F32)).astype(BF16)
    sums = jnp.dot(jnp.concatenate([high, mid, low], axis=0), upper, preferred_element_type=F32)
    sums = sums[0:8] + sums[8:16] + sums[16:24]
    cum_row = sums[0:1, :]
    rows = jnp.concatenate([cum_row, rates, jnp.zeros((D - 2, D), F32)], axis=0)
    cols = rows.T
    cum_col = jnp.broadcast_to(cols[:, 0:1], (D, D))
    rate_col = jnp.broadcast_to(cols[:, 1:2], (D, D))
    spread = cum_col - cum_row
    inclusive = row >= col
    within = jnp.where(inclusive, jnp.exp(jnp.where(inclusive, spread, 0.0)), 0.0)
    keys_t = keys.T
    both = product(jnp.concatenate([left(query), left(keys)], axis=0), right(keys_t))
    query_key, key_key = both[:D], both[D:]
    scores = within * query_key
    system = jnp.where(row > col, rate_col * within * key_key, 0.0)
    differ = row ^ col
    inverse = jnp.where(row == col, 1.0, jnp.where(differ == 1, -system, 0.0))
    for level in range(1, 7):
        part = jnp.where((differ >= (1 << level)) & (differ < (2 << level)), system, 0.0)
        inner = product(left(part), right(inverse))
        inverse = inverse - product(left(inverse), right(inner))
    growth = jnp.exp(cum_col)
    targets = jnp.concatenate([(rate_col * growth) * keys, rate_col * values], axis=1)
    solved = product(left(inverse), right(targets))
    solved_right = right(solved)
    tail_row = jnp.exp(cum_col[D - 1 : D, :] - cum_row)
    weighted_t = keys_t * tail_row
    inside = product(left(weighted_t), solved_right)
    whole = jnp.where(row == col, growth[D - 1 : D, :], 0.0)
    maps = jnp.concatenate([whole - inside[:, :D], inside[:, D:]], axis=1)
    seen = product(left(scores), solved_right)
    response = growth * query - seen[:, :D]
    return maps, response, seen[:, D:]


def compose(later, earlier):
    joined = product(left(later[:, :D]), right(earlier))
    return jnp.concatenate([joined[:, :D], joined[:, D:] + later[:, D:]], axis=1)


def kernel(
    q_ref, k_ref, v_ref, z_ref, gate_ref, cq_ref, ck_ref, cv_ref, gain_ref, w_ref, out_ref,
    raw, gates, halo, ext, act, maps, resp, direct, mine, got, own, back, whole, w_all, x_send, x_got,
    send_raw, recv_raw, send_gate, recv_gate, send_halo, recv_halo, send_z, recv_z,
    send_back, recv_back, send_x, recv_x, w_sem,
):
    me, head = lax.axis_index("seq"), lax.axis_index("head")
    plane, place = me // PLANE, lax.rem(me, PLANE)
    first = plane * PLANE

    def peer(r):
        return lax.rem(place + r, PLANE)

    def plane_at(r):
        return lax.rem(plane + r + PLANES, PLANES) * PLANE + place

    barrier = pltpu.get_barrier_semaphore()
    near = [(first + peer(r), head) for r in range(1, PLANE)]
    near += [(plane_at(r), head) for r in (1, -1, 2, -2, 4)]
    near += [(me, lax.rem(head + r, HEADS_X)) for r in range(1, HEADS_X)]
    for device in near:
        pl.semaphore_signal(barrier, inc=1, device_id=device, device_id_type=MESH)

    w_copy = pltpu.make_async_copy(w_ref, w_all, w_sem)
    w_copy.start()
    sources = (k_ref, q_ref, v_ref, z_ref)

    def columns(a, dest):
        return pl.ds(pl.multiple_of((dest // 2 if a < 2 else dest) * D, D), D)

    kept = []
    for a in range(4):
        copy = pltpu.make_async_copy(
            sources[a].at[:, columns(a, place)], raw.at[a, place], recv_raw.at[a, place]
        )
        copy.start()
        kept.append(copy)
    gates[place] = gate_ref[place]

    pl.semaphore_wait(barrier, len(near))

    sent = []

    def send(src, dst, send_sem, recv_sem, device):
        copy = pltpu.make_async_remote_copy(
            src_ref=src, dst_ref=dst, send_sem=send_sem, recv_sem=recv_sem, device_id=device, device_id_type=MESH
        )
        copy.start()
        sent.append(copy)
        return copy

    def arrived(dst, send_sem, recv_sem):
        pltpu.make_async_remote_copy(
            src_ref=dst, dst_ref=dst, send_sem=send_sem, recv_sem=recv_sem, device_id=near[0], device_id_type=MESH
        ).wait_recv()

    for a in range(4):
        for r in range(1, PLANE):
            dest = peer(r)
            send(
                sources[a].at[:, columns(a, dest)], raw.at[a, place],
                send_raw.at[a, r - 1], recv_raw.at[a, place], (first + dest, head),
            )
        if a == 0:
            for r in range(1, PLANE):
                dest = peer(r)
                send(
                    gate_ref.at[dest], gates.at[place],
                    send_gate.at[r - 1], recv_gate.at[place], (first + dest, head),
                )

    taps = [
        ck_ref[:, columns(0, place)],
        cq_ref[:, columns(0, place)],
        cv_ref[:, columns(2, place)],
    ]

    def activate(a, before, now):
        ext[a, 0:8, :] = before.astype(F32)[8:16]
        ext[a, 8 : 8 + D, :] = now.astype(F32)
        total = taps[a][0:1] * ext[a, 5 : 5 + D, :]
        for t in range(1, 4):
            total = total + taps[a][t : t + 1] * ext[a, 5 + t : 5 + t + D, :]
        total = silu(total)
        if a < 2:
            total = total * lax.rsqrt(jnp.sum(total * total, axis=-1, keepdims=True) + 1e-06)
        if a == 1:
            total = total * D ** (-0.5)
        return total

    for a in range(4):
        kept[a].wait()
    for a in range(3):
        for r in range(1, PLANE):
            src = peer(r)
            arrived(raw.at[a, src], send_raw.at[a, 0], recv_raw.at[a, src])
        send(
            raw.at[a, PLANE - 1, D - 16 : D, :], halo.at[a], send_halo.at[a], recv_halo.at[a], (plane_at(1), head)
        )

    @pl.loop(1, PLANE)
    def _(n):
        for a in range(3):
            act[a, n] = activate(a, raw[a, n - 1, D - 16 : D, :], raw[a, n])

    for a in range(3):
        arrived(halo.at[a], send_halo.at[a], recv_halo.at[a])
        before = jnp.where(plane > 0, halo[a], jnp.zeros_like(halo[a]))
        act[a, 0] = activate(a, before, raw[a, 0])
    for r in range(1, PLANE):
        src = peer(r)
        arrived(gates.at[src], send_gate.at[0], recv_gate.at[src])

    @pl.loop(0, PLANE // 4)
    def _(t):
        for u in range(4):
            n = t * 4 + u
            maps[n], resp[n], direct[n] = chunk_maps(act[1, n], act[0, n], act[2, n], gates[n])

    joined = {}
    joined[0, 1] = compose(maps[1], maps[0])
    joined[2, 3] = compose(maps[3], maps[2])
    joined[4, 5] = compose(maps[5], maps[4])
    joined[6, 7] = compose(maps[7], maps[6])
    joined[0, 3] = compose(joined[2, 3], joined[0, 1])
    joined[4, 7] = compose(joined[6, 7], joined[4, 5])
    total = compose(joined[4, 7], joined[0, 3])

    mine[0] = total
    send(mine.at[0], got.at[0], send_z.at[0], recv_z.at[0], (plane_at(1), head))

    prefix = [None, maps[0], joined[0, 1], compose(maps[2], joined[0, 1]), joined[0, 3]]
    prefix.append(compose(maps[4], joined[0, 3]))
    prefix.append(compose(joined[4, 5], joined[0, 3]))
    prefix.append(compose(maps[6], prefix[6]))
    for n in range(1, PLANE):
        through = product(left(resp[n]), right(prefix[n]))
        resp[n] = through[:, :D]
        direct[n] = through[:, D:] + direct[n]

    def reached(slot, distance):
        arrived(got.at[slot], send_z.at[slot], recv_z.at[slot])
        return jnp.where(plane >= distance, got[slot], jnp.zeros_like(got[slot]))

    one = reached(0, 1)
    two = compose(total, one)
    mine[1] = two
    send(mine.at[1], got.at[1], send_z.at[1], recv_z.at[1], (plane_at(2), head))

    for r in range(1, PLANE):
        src = peer(r)
        arrived(raw.at[3, src], send_raw.at[3, 0], recv_raw.at[3, src])

    @pl.loop(0, PLANE)
    def _(n):
        own[n] = silu(raw[3, n].astype(F32)) * gain_ref[...]

    before = reached(1, 2)
    four = product(left(two[:, :D]), right(before[:, D:])) + two[:, D:]
    mine[2, :, 0:D] = four
    send(
        mine.at[2, :, pl.ds(0, D)], got.at[2, :, pl.ds(0, D)], send_z.at[2], recv_z.at[2], (plane_at(4), head)
    )
    three = compose(one, before)
    arrived(got.at[2, :, pl.ds(0, D)], send_z.at[2], recv_z.at[2])
    far = jnp.where(plane >= 4, got[2, :, 0:D], 0.0)
    state = product(left(three[:, :D]), right(far)) + three[:, D:]
    state_right = right(state)

    for r in range(PLANE - 1, -1, -1):
        n = peer(r)
        heads_out = product(left(resp[n]), state_right) + direct[n]
        scale = lax.rsqrt(jnp.mean(heads_out * heads_out, axis=-1, keepdims=True) + 1e-06)
        gated = (heads_out * scale * own[n]).astype(BF16)
        lanes = pl.ds(pl.multiple_of(place * D, D), D)
        if r == 0:
            whole[:, lanes] = gated
        else:
            back[r - 1] = gated
            send(
                back.at[r - 1], whole.at[:, lanes], send_back.at[r - 1], recv_back.at[place], (first + n, head)
            )
    for r in range(1, PLANE):
        src = peer(r)
        arrived(whole.at[:, pl.ds(pl.multiple_of(src * D, D), D)], send_back.at[0], recv_back.at[src])
    w_copy.wait()

    width = out_ref.shape[1]
    for r in (2, 1, 3, 0):
        dest = lax.rem(head + r, HEADS_X)
        weights = w_all[:, pl.ds(pl.multiple_of(dest * width, width), width)]
        share = jnp.dot(whole[...], weights, preferred_element_type=F32)
        if r > 0:
            x_send[r - 1] = share.astype(BF16)
            send(x_send.at[r - 1], x_got.at[r - 1], send_x.at[r - 1], recv_x.at[r - 1], (me, dest))
    for r in (1, 3, 2):
        arrived(x_got.at[r - 1], send_x.at[r - 1], recv_x.at[r - 1])
        share = share + x_got[r - 1].astype(F32)
    out_ref[...] = share.astype(BF16)
    for copy in sent:
        copy.wait_send()


def on_device(q_in, k_in, v_in, z_gate, decay, rate, conv_q, conv_k, conv_v, norm_gain, w_out):
    heads = decay.shape[1]
    gate = jnp.stack([decay.T, rate.T] + [jnp.zeros((heads, D), F32)] * 6, axis=1)
    tok, width = q_in.shape
    any_space = pl.BlockSpec(memory_space=pl.ANY)
    vmem = pl.BlockSpec(memory_space=VMEM)
    dma = pltpu.SemaphoreType.DMA
    return pl.pallas_call(
        kernel,
        out_shape=jax.ShapeDtypeStruct((tok, width), BF16),
        in_specs=[any_space] * 4 + [vmem] * 5 + [any_space],
        out_specs=vmem,
        scratch_shapes=[
            VMEM((4, PLANE, D, D), BF16),
            VMEM((PLANE, 8, D), F32),
            VMEM((3, 16, D), BF16),
            VMEM((3, D + 8, D), F32),
            VMEM((3, PLANE, D, D), F32),
            VMEM((PLANE, D, 2 * D), F32),
            VMEM((PLANE, D, D), F32),
            VMEM((PLANE, D, D), F32),
            VMEM((3, D, 2 * D), F32),
            VMEM((3, D, 2 * D), F32),
            VMEM((PLANE, D, D), F32),
            VMEM((PLANE - 1, D, D), BF16),
            VMEM((tok, PLANE * D), BF16),
            VMEM(w_out.shape, BF16),
            VMEM((HEADS_X - 1, tok, width), BF16),
            VMEM((HEADS_X - 1, tok, width), BF16),
            dma((4, PLANE - 1)), dma((4, PLANE)),
            dma((PLANE - 1,)), dma((PLANE,)),
            dma((3,)), dma((3,)),
            dma((3,)), dma((3,)),
            dma((PLANE - 1,)), dma((PLANE,)),
            dma((HEADS_X - 1,)), dma((HEADS_X - 1,)),
            dma,
        ],
        compiler_params=pltpu.CompilerParams(
            collective_id=0, has_side_effects=True, vmem_limit_bytes=40 * 1024 * 1024
        ),
    )(q_in, k_in, v_in, z_gate, gate, conv_q, conv_k, conv_v, norm_gain.reshape(1, D), w_out)


def solution(mesh):
    return jax.shard_map(
        on_device,
        mesh=mesh,
        in_specs=(
            P("seq", "head"),
            P("seq", "head"),
            P("seq", "head"),
            P("seq", "head"),
            P("seq", "head"),
            P("seq", "head"),
            P(None, "head"),
            P(None, "head"),
            P(None, "head"),
            P(),
            P("head", None),
        ),
        out_specs=P("seq", "head"),
        check_vma=False,
    )
```

```python
import jax
import jax.numpy as jnp
from jax import lax
from jax.experimental import pallas as pl
from jax.experimental.pallas import tpu as pltpu
from jax.sharding import PartitionSpec as P

F32 = jnp.float32
BF16 = jnp.bfloat16
D = 128
PLANE = 8
PLANES = 8
HEADS_X = 4
MESH = pl.DeviceIdType.MESH
VMEM = pltpu.VMEM


def split(x):
    high = x.astype(BF16)
    return high, (x - high.astype(F32)).astype(BF16)


def left(x):
    high, low = split(x)
    return jnp.concatenate([high, low], axis=1)


def right(x):
    high, low = split(x)
    both = jnp.concatenate([high, low], axis=1)
    return jnp.concatenate([both, both], axis=0)


def product(lhs, rhs):
    both = jnp.dot(lhs, rhs, preferred_element_type=F32)
    half = both.shape[1] // 2
    return both[:, :half] + both[:, half:]


def silu(x):
    return x / (1.0 + jnp.exp(-x))


def iotas(rows=D):
    return lax.broadcasted_iota(jnp.int32, (rows, D), 0), lax.broadcasted_iota(jnp.int32, (rows, D), 1)


def gate_tables(decays, rates):
    row, col = iotas()
    upper = (row <= col).astype(BF16)
    high, rest = split(decays)
    mid, low = split(decays - high.astype(F32))
    sums = jnp.dot(jnp.concatenate([high, mid, low], axis=0), upper, preferred_element_type=F32)
    sums = sums[0:PLANE] + sums[PLANE : 2 * PLANE] + sums[2 * PLANE : 3 * PLANE]
    table = jnp.concatenate([sums, rates, jnp.zeros((D - 2 * PLANE, D), F32)], axis=0)
    return sums, table.T


def inverses(systems):
    row, col = iotas()
    count = len(systems)
    diagonal = (row >> 4) == (col >> 4)
    packed = []
    for system in systems:
        blocks = jnp.where(diagonal, system, 0.0)
        rows = blocks[0:16]
        for b in range(1, 8):
            rows = rows + blocks[16 * b : 16 * b + 16]
        packed.append(rows)
    packed = left(jnp.concatenate(packed, axis=0))
    row16, col16 = iotas(16)
    eye = jnp.where(row16 == (col16 & 15), 1.0, 0.0)
    found = jnp.concatenate([eye] * count, axis=0).reshape(count, 16, D)
    same = (row >> 4) == (col >> 4)
    for first in range(0, 15, 2):
        picks = range(first, min(first + 2, 15))
        spread = [(same & ((row & 15) == j)).astype(BF16) for j in picks]
        spread = jnp.concatenate(spread, axis=1)
        spread = jnp.dot(packed, jnp.concatenate([spread, spread], axis=0), preferred_element_type=F32)
        for u, j in enumerate(picks):
            factor = spread[:, u * D : (u + 1) * D].reshape(count, 16, D)
            found = found - factor * found[:, j : j + 1, :]
    result = [jnp.where(diagonal, jnp.concatenate([found[n]] * 8, axis=0), 0.0) for n in range(count)]
    differ = row ^ col
    for level in range(4, 7):
        off = (differ >= (1 << level)) & (differ < (2 << level))
        parts = [left(jnp.where(off, system, 0.0)) for system in systems]
        inner = [product(parts[n], right(result[n])) for n in range(count)]
        result = [result[n] - product(left(result[n]), right(inner[n])) for n in range(count)]
    return result


def compose(later, earlier):
    d_later, both_later = later
    d_earlier, both_earlier = earlier
    joined = product(left(both_later[:, :D]), right(both_earlier))
    wide = jnp.concatenate([d_later, d_later], axis=1)
    factors = jnp.concatenate([d_earlier, jnp.ones_like(d_earlier)], axis=1)
    return d_later * d_earlier, joined + wide * both_earlier + factors * both_later


def kernel(
    q_ref, k_ref, v_ref, z_ref, decay_ref, rate_ref, cq_ref, ck_ref, cv_ref, gain_ref, w_ref, out_ref,
    raw, gate_own, gates, halo, ext, act, taps, gain, reach, direct, mine, got, own, back, whole, w_all, x_send, x_got,
    send_raw, recv_raw, send_gate, recv_gate, send_halo, recv_halo, send_z, recv_z,
    send_back, recv_back, send_x, recv_x, w_sem, small_sem,
):
    me, head = lax.axis_index("seq"), lax.axis_index("head")
    plane, place = me // PLANE, lax.rem(me, PLANE)
    first = plane * PLANE
    last = place == PLANE - 1

    def peer(r):
        return lax.rem(place + r, PLANE)

    def plane_at(r):
        return lax.rem(plane + r + PLANES, PLANES) * PLANE

    sources = (k_ref, v_ref, q_ref, z_ref)

    def columns(a, dest):
        return pl.ds(pl.multiple_of((dest if a % 2 else dest // 2) * D, D), D)

    small = [
        pltpu.make_async_copy(src, dst, small_sem.at[i])
        for i, (src, dst) in enumerate(
            [
                (decay_ref, gate_own.at[0:8]),
                (rate_ref, gate_own.at[8:16]),
                (ck_ref.at[:, columns(0, place)], taps.at[0]),
                (cv_ref.at[:, columns(1, place)], taps.at[1]),
                (cq_ref.at[:, columns(2, place)], taps.at[2]),
                (gain_ref, gain),
            ]
        )
    ]
    for copy in small:
        copy.start()

    barrier = pltpu.get_barrier_semaphore()
    near = [(first + peer(r), head) for r in range(1, PLANE)]
    near += [(plane_at(r) + place, head) for r in (1, -1, 2, -2, 4)]
    near += [(me, lax.rem(head + r, HEADS_X)) for r in range(1, HEADS_X)]
    for device in near:
        pl.semaphore_signal(barrier, inc=1, device_id=device, device_id_type=MESH)

    @pl.when(jnp.logical_not(last))
    def _():
        pl.semaphore_signal(barrier, inc=1, device_id=(plane_at(-1) + PLANE - 1, head), device_id_type=MESH)

    kept = []
    for a in range(4):
        copy = pltpu.make_async_copy(
            sources[a].at[:, columns(a, place)], raw.at[a, place], recv_raw.at[a, place]
        )
        copy.start()
        kept.append(copy)
    w_copy = pltpu.make_async_copy(w_ref, w_all, w_sem)
    w_copy.start()
    for copy in small[:2]:
        copy.wait()

    pl.semaphore_wait(barrier, len(near) + jnp.where(last, PLANE - 1, 0))

    sent = []

    def remote(src, dst, send_sem, recv_sem, device):
        return pltpu.make_async_remote_copy(
            src_ref=src, dst_ref=dst, send_sem=send_sem, recv_sem=recv_sem, device_id=device, device_id_type=MESH
        )

    def send(*args):
        copy = remote(*args)
        copy.start()
        sent.append(copy)

    def arrived(dst, send_sem, recv_sem):
        remote(dst, dst, send_sem, recv_sem, near[0]).wait_recv()

    def halo_copy(a, j):
        return remote(
            sources[a].at[D - 16 : D, columns(a, j)], halo.at[a],
            send_halo.at[a, j], recv_halo.at[a], (plane_at(1) + j, head),
        )

    for r in range(1, PLANE):
        dest = peer(r)
        send(gate_own, gates.at[place], send_gate.at[r - 1], recv_gate.at[place], (first + dest, head))
    for a in range(4):
        for r in range(1, PLANE):
            dest = peer(r)
            send(
                sources[a].at[:, columns(a, dest)], raw.at[a, place],
                send_raw.at[a, r - 1], recv_raw.at[a, place], (first + dest, head),
            )
        if a < 3:

            @pl.when(last)
            def _():
                for j in range(PLANE):
                    halo_copy(a, j).start()

    def raw_arrived(a):
        kept[a].wait()
        for r in range(1, PLANE):
            src = peer(r)
            arrived(raw.at[a, src], send_raw.at[a, 0], recv_raw.at[a, src])
        if a < 3:
            arrived(halo.at[a], send_halo.at[a, 0], recv_halo.at[a])

    def activate(a):
        before = jnp.where(plane > 0, halo[a].astype(F32), 0.0)
        ext[a, 0:8, :] = before[8:16]
        for n in range(PLANE):
            ext[a, 8 + n * D : 8 + (n + 1) * D, :] = raw[a, n].astype(F32)
        for n in range(PLANE):
            total = taps[a, 0:1] * ext[a, 5 + n * D : 5 + (n + 1) * D, :]
            for t in range(1, 4):
                total = total + taps[a, t : t + 1] * ext[a, 5 + t + n * D : 5 + t + (n + 1) * D, :]
            total = silu(total)
            if a != 1:
                total = total * lax.rsqrt(jnp.sum(total * total, axis=-1, keepdims=True) + 1e-06)
            if a == 2:
                total = total * D ** (-0.5)
            act[a, n] = total

    gates[place] = gate_own[...]
    for r in range(1, PLANE):
        src = peer(r)
        arrived(gates.at[src], send_gate.at[0], recv_gate.at[src])
    chunks = range(PLANE)
    decays = jnp.concatenate([gates[n, pl.ds(place, 1), :] for n in chunks], axis=0)
    rates = jnp.concatenate([gates[n, pl.ds(place + PLANE, 1), :] for n in chunks], axis=0)
    cum_rows, table = gate_tables(decays, rates)
    row, col = iotas()
    inclusive = row >= col
    cum_col = [jnp.broadcast_to(table[:, n : n + 1], (D, D)) for n in chunks]
    rate_col = [jnp.broadcast_to(table[:, PLANE + n : PLANE + n + 1], (D, D)) for n in chunks]
    within = []
    for n in chunks:
        spread = cum_col[n] - cum_rows[n : n + 1]
        within.append(jnp.where(inclusive, jnp.exp(jnp.where(inclusive, spread, 0.0)), 0.0))
    growth = [jnp.exp(cum_col[n]) for n in chunks]
    tail = [jnp.exp(cum_col[n][D - 1 : D, :] - cum_rows[n : n + 1]) for n in chunks]
    for copy in small[2:]:
        copy.wait()

    raw_arrived(0)
    activate(0)
    keys = [act[0, n] for n in chunks]
    keys_t = [keys[n].T for n in chunks]
    keys_right = [right(keys_t[n]) for n in chunks]
    key_key = [product(left(keys[n]), keys_right[n]) for n in chunks]
    systems = [jnp.where(row > col, rate_col[n] * within[n] * key_key[n], 0.0) for n in chunks]
    inverse = [left(x) for x in inverses(systems)]
    weighted = [left(keys_t[n] * tail[n]) for n in chunks]

    raw_arrived(1)
    activate(1)
    targets = [
        right(jnp.concatenate([(rate_col[n] * growth[n]) * keys[n], rate_col[n] * act[1, n]], axis=1)) for n in chunks
    ]
    solved = [right(product(inverse[n], targets[n])) for n in chunks]
    sign = jnp.concatenate([jnp.full((1, D), -1.0, F32), jnp.ones((1, D), F32)], axis=1)
    maps = [(growth[n][D - 1 : D, :], sign * product(weighted[n], solved[n])) for n in chunks]

    two = [compose(maps[n + 1], maps[n]) for n in range(0, PLANE, 2)]
    four = [compose(two[n + 1], two[n]) for n in range(0, PLANE // 2, 2)]
    total = compose(four[1], four[0])

    row16, _ = iotas(16)

    def put(slot, stretch, distance):
        d, both = stretch
        mine[slot, 0:D, :] = both.astype(BF16)
        high, rest = split(d)
        mid, low = split(d - high.astype(F32))
        digits = jnp.where(row16 == 0, high.astype(F32), jnp.where(row16 == 1, mid.astype(F32), low.astype(F32)))
        mine[slot, D : D + 16, 0:D] = jnp.where(row16 < 3, digits, 0.0).astype(BF16)
        mine[slot, D : D + 16, D : 2 * D] = jnp.zeros((16, D), BF16)
        send(mine.at[slot], got.at[slot], send_z.at[slot], recv_z.at[slot], (plane_at(distance) + place, head))

    def take(slot, distance):
        arrived(got.at[slot], send_z.at[slot], recv_z.at[slot])
        held = jnp.where(plane >= distance, got[slot].astype(F32), 0.0)
        return jnp.sum(held[D : D + 16, 0:D], axis=0, keepdims=True), held[0:D]

    put(0, total, 1)

    raw_arrived(2)
    activate(2)
    queries = [act[2, n] for n in chunks]
    scores = [left(within[n] * product(left(queries[n]), keys_right[n])) for n in chunks]
    seen = [product(scores[n], solved[n]) for n in chunks]
    response = [growth[n] * queries[n] - seen[n][:, :D] for n in chunks]
    prefix = {1: maps[0], 2: two[0], 4: four[0]}
    prefix[3] = compose(maps[2], two[0])
    prefix[5] = compose(maps[4], four[0])
    prefix[6] = compose(two[2], four[0])
    reach[0] = left(response[0])
    direct[0] = seen[0][:, D:]

    def reach_of(n):
        through = product(left(response[n]), right(prefix[n][1]))
        reach[n] = left(through[:, :D] + prefix[n][0] * response[n])
        direct[n] = through[:, D:] + seen[n][:, D:]

    one = take(0, 1)
    pair = compose(total, one)
    put(1, pair, 2)
    prefix[7] = compose(maps[6], prefix[6])
    for n in range(1, PLANE):
        reach_of(n)
    raw_arrived(3)
    for n in chunks:
        own[n] = silu(raw[3, n].astype(F32)) * gain[...]

    before = take(1, 2)
    mine[2, 0:D, 0:D] = compose(pair, before)[1][:, D:].astype(BF16)
    send(
        mine.at[2, 0:D, 0:D], got.at[2, 0:D, 0:D], send_z.at[2], recv_z.at[2], (plane_at(4) + place, head)
    )
    three = compose(one, before)
    arrived(got.at[2, 0:D, 0:D], send_z.at[2], recv_z.at[2])
    far = jnp.where(plane >= 4, got[2, 0:D, 0:D].astype(F32), 0.0)
    state = product(left(three[1][:, :D]), right(far)) + three[0] * far + three[1][:, D:]
    state = right(state)

    lanes = pl.ds(pl.multiple_of(place * D, D), D)
    halves = [slice(0, D // 2), slice(D // 2, D)]
    for h, rows in enumerate(halves):
        for n in chunks:
            heads_out = product(reach[n, rows, :], state) + direct[n, rows, :]
            scale = lax.rsqrt(jnp.mean(heads_out * heads_out, axis=-1, keepdims=True) + 1e-06)
            back[n, rows, :] = (heads_out * scale * own[n, rows, :]).astype(BF16)
        for r in range(1, PLANE):
            dest = peer(r)
            send(
                back.at[dest, rows, :], whole.at[rows, lanes],
                send_back.at[h, r - 1], recv_back.at[h, place], (first + dest, head),
            )
    whole[:, lanes] = back[place]
    w_copy.wait()

    width = out_ref.shape[1]
    for h, rows in enumerate(halves):
        for r in range(1, PLANE):
            src = peer(r)
            arrived(
                whole.at[rows, pl.ds(pl.multiple_of(src * D, D), D)], send_back.at[h, 0], recv_back.at[h, src]
            )
        for r in (2, 1, 3):
            dest = lax.rem(head + r, HEADS_X)
            weights = w_all[:, pl.ds(pl.multiple_of(dest * width, width), width)]
            x_send[r - 1, rows, :] = jnp.dot(whole[rows, :], weights, preferred_element_type=F32).astype(BF16)
            send(
                x_send.at[r - 1, rows, :], x_got.at[r - 1, rows, :],
                send_x.at[h, r - 1], recv_x.at[h, r - 1], (me, dest),
            )
    weights = w_all[:, pl.ds(pl.multiple_of(head * width, width), width)]
    share = jnp.dot(whole[...], weights, preferred_element_type=F32)
    for h, rows in enumerate(halves):
        part = share[rows]
        for r in (1, 3, 2):
            arrived(x_got.at[r - 1, rows, :], send_x.at[h, r - 1], recv_x.at[h, r - 1])
            part = part + x_got[r - 1, rows, :].astype(F32)
        out_ref[rows, :] = part.astype(BF16)
    for copy in sent:
        copy.wait_send()

    @pl.when(last)
    def _():
        for a in range(3):
            for j in range(PLANE):
                halo_copy(a, j).wait_send()


def on_device(q_in, k_in, v_in, z_gate, decay, rate, conv_q, conv_k, conv_v, norm_gain, w_out):
    tok, width = q_in.shape
    dma = pltpu.SemaphoreType.DMA
    return pl.pallas_call(
        kernel,
        out_shape=jax.ShapeDtypeStruct((tok, width), BF16),
        in_specs=[pl.BlockSpec(memory_space=pltpu.HBM)] * 11,
        out_specs=pl.BlockSpec(memory_space=VMEM),
        scratch_shapes=[
            VMEM((4, PLANE, D, D), BF16),
            VMEM((2 * PLANE, D), F32),
            VMEM((PLANE, 2 * PLANE, D), F32),
            VMEM((3, 16, D), BF16),
            VMEM((3, PLANE * D + 8, D), F32),
            VMEM((3, PLANE, D, D), F32),
            VMEM((3, 4, D), F32),
            VMEM((1, D), F32),
            VMEM((PLANE, D, 2 * D), BF16),
            VMEM((PLANE, D, D), F32),
            VMEM((3, D + 16, 2 * D), BF16),
            VMEM((3, D + 16, 2 * D), BF16),
            VMEM((PLANE, D, D), F32),
            VMEM((PLANE, D, D), BF16),
            VMEM((tok, PLANE * D), BF16),
            VMEM(w_out.shape, BF16),
            VMEM((HEADS_X - 1, tok, width), BF16),
            VMEM((HEADS_X - 1, tok, width), BF16),
            dma((4, PLANE - 1)), dma((4, PLANE)),
            dma((PLANE - 1,)), dma((PLANE,)),
            dma((3, PLANE)), dma((3,)),
            dma((3,)), dma((3,)),
            dma((2, PLANE - 1)), dma((2, PLANE)),
            dma((2, HEADS_X - 1)), dma((2, HEADS_X - 1)),
            dma, dma((6,)),
        ],
        compiler_params=pltpu.CompilerParams(
            collective_id=0, has_side_effects=True, vmem_limit_bytes=48 * 1024 * 1024
        ),
    )(q_in, k_in, v_in, z_gate, decay.T, rate.T, conv_q, conv_k, conv_v, norm_gain.reshape(1, D), w_out)


def solution(mesh):
    return jax.shard_map(
        on_device,
        mesh=mesh,
        in_specs=(
            P("seq", "head"),
            P("seq", "head"),
            P("seq", "head"),
            P("seq", "head"),
            P("seq", "head"),
            P("seq", "head"),
            P(None, "head"),
            P(None, "head"),
            P(None, "head"),
            P(),
            P("head", None),
        ),
        out_specs=P("seq", "head"),
        check_vma=False,
    )
```

```python
import jax
import jax.numpy as jnp
from jax import lax
from jax.experimental import pallas as pl
from jax.experimental.pallas import tpu as pltpu
from jax.sharding import PartitionSpec as P

F32 = jnp.float32
BF16 = jnp.bfloat16
D = 128
PLANE = 8
PLANES = 8
HEADS_X = 4
PIECES = 2
MESH = pl.DeviceIdType.MESH
VMEM = pltpu.VMEM


def split(x):
    high = x.astype(BF16)
    return high, (x - high.astype(F32)).astype(BF16)


def left(x):
    high, low = split(x)
    return jnp.concatenate([high, low], axis=1)


def right(x):
    high, low = split(x)
    both = jnp.concatenate([high, low], axis=1)
    return jnp.concatenate([both, both], axis=0)


def product(lhs, rhs, count=1):
    both = jnp.dot(lhs, rhs, preferred_element_type=F32)
    half = both.shape[1] // (2 * count)
    parts = [both[:, 2 * i * half : (2 * i + 1) * half] + both[:, (2 * i + 1) * half : (2 * i + 2) * half] for i in range(count)]
    return parts[0] if count == 1 else jnp.concatenate(parts, axis=1)


def silu(x):
    return x / (1.0 + jnp.exp(-x))


def iotas(rows=D):
    return lax.broadcasted_iota(jnp.int32, (rows, D), 0), lax.broadcasted_iota(jnp.int32, (rows, D), 1)


def gate_tables(decays, rates):
    row, col = iotas()
    upper = (row <= col).astype(BF16)
    high, rest = split(decays)
    mid, low = split(decays - high.astype(F32))
    sums = jnp.dot(jnp.concatenate([high, mid, low], axis=0), upper, preferred_element_type=F32)
    sums = sums[0:PLANE] + sums[PLANE : 2 * PLANE] + sums[2 * PLANE : 3 * PLANE]
    table = jnp.concatenate([sums, rates, jnp.zeros((D - 2 * PLANE, D), F32)], axis=0)
    return sums, table.T


def inverses(systems):
    row, col = iotas()
    count = len(systems)
    diagonal = (row >> 4) == (col >> 4)
    packed = []
    for system in systems:
        blocks = jnp.where(diagonal, system, 0.0)
        rows = blocks[0:16]
        for b in range(1, 8):
            rows = rows + blocks[16 * b : 16 * b + 16]
        packed.append(rows)
    packed = left(jnp.concatenate(packed, axis=0))
    row16, col16 = iotas(16)
    eye = jnp.where(row16 == (col16 & 15), 1.0, 0.0)
    found = jnp.concatenate([eye] * count, axis=0).reshape(count, 16, D)
    same = (row >> 4) == (col >> 4)
    for first in range(0, 15, 2):
        picks = range(first, min(first + 2, 15))
        spread = [(same & ((row & 15) == j)).astype(BF16) for j in picks]
        spread = jnp.concatenate(spread, axis=1)
        spread = jnp.dot(packed, jnp.concatenate([spread, spread], axis=0), preferred_element_type=F32)
        for u, j in enumerate(picks):
            factor = spread[:, u * D : (u + 1) * D].reshape(count, 16, D)
            found = found - factor * found[:, j : j + 1, :]
    result = [jnp.where(diagonal, jnp.concatenate([found[n]] * 8, axis=0), 0.0) for n in range(count)]
    differ = row ^ col
    for level in range(4, 7):
        off = (differ >= (1 << level)) & (differ < (2 << level))
        parts = [left(jnp.where(off, system, 0.0)) for system in systems]
        inner = [product(parts[n], right(result[n])) for n in range(count)]
        result = [result[n] - product(left(result[n]), right(inner[n])) for n in range(count)]
    return result


def product_once(linear, b):
    whole = jnp.dot(linear[2], jnp.concatenate([b, b], axis=0), preferred_element_type=F32)
    return whole + linear[0] * b.astype(F32)


def join(later, earlier):
    d_later, m_later, split_later = later
    d_earlier, m_earlier, _ = earlier
    m = product(split_later, right(m_earlier)) + d_later * m_earlier + d_earlier * m_later
    return d_later * d_earlier, m, left(m)


def advance(later, b_later, b_earlier):
    return product(later[2], right(b_earlier)) + later[0] * b_earlier + b_later


def kernel(
    q_ref, k_ref, v_ref, z_ref, decay_ref, rate_ref, cq_ref, ck_ref, cv_ref, gain_ref, w_ref, out_ref,
    blocks, raw, gate_own, gate_tiles, gates, halo, ext, act, taps, gain, reach, direct,
    mine_m, got_m, mine_b, got_b, own, back, whole, w_all, x_send, x_got,
    send_raw, recv_raw, send_gate, recv_gate, send_halo, recv_halo, send_m, recv_m, send_b, recv_b,
    send_back, recv_back, send_x, recv_x, w_sem, small_sem, block_sem, known,
):
    me, head = lax.axis_index("seq"), lax.axis_index("head")
    plane, place = me // PLANE, lax.rem(me, PLANE)
    first = plane * PLANE
    last = place == PLANE - 1

    def peer(r):
        return lax.rem(place + r, PLANE)

    def plane_at(r):
        return lax.rem(plane + r + PLANES, PLANES) * PLANE

    sources = (k_ref, v_ref, q_ref, z_ref)

    def columns(a, dest):
        return pl.ds(pl.multiple_of((dest if a % 2 else dest // 2) * D, D), D)

    small = [
        pltpu.make_async_copy(src, dst, small_sem.at[i])
        for i, (src, dst) in enumerate(
            [
                (decay_ref, gate_own.at[0:8]),
                (rate_ref, gate_own.at[8:16]),
                (ck_ref.at[:, columns(0, place)], taps.at[0]),
                (cv_ref.at[:, columns(1, place)], taps.at[1]),
                (cq_ref.at[:, columns(2, place)], taps.at[2]),
                (gain_ref, gain),
            ]
        )
    ]
    for copy in small:
        copy.start()

    barrier = pltpu.get_barrier_semaphore()
    near = [(first + peer(r), head) for r in range(1, PLANE)]
    near += [(me, lax.rem(head + r, HEADS_X)) for r in range(1, HEADS_X)]
    for device in near:
        pl.semaphore_signal(barrier, inc=1, device_id=device, device_id_type=MESH)

    def tell(sem, r):
        pl.semaphore_signal(sem, inc=1, device_id=(plane_at(r) + place, head), device_id_type=MESH)

    @pl.when(plane > 0)
    def _():
        tell(barrier, -1)

        @pl.when(jnp.logical_not(last))
        def _():
            pl.semaphore_signal(barrier, inc=1, device_id=(plane_at(-1) + PLANE - 1, head), device_id_type=MESH)

    local = []
    kept = []
    for a in range(4):
        for b in range(PLANE if a % 2 else PLANE // 2):
            copy = pltpu.make_async_copy(
                sources[a].at[:, b * D : (b + 1) * D], blocks.at[a, b], block_sem.at[a, b]
            )
            copy.start()
            local.append((a, copy))
        copy = pltpu.make_async_copy(
            sources[a].at[:, columns(a, place)], raw.at[a, place], recv_raw.at[a, place]
        )
        copy.start()
        kept.append(copy)
    w_copy = pltpu.make_async_copy(w_ref, w_all, w_sem)
    w_copy.start()
    for copy in small[:2]:
        copy.wait()
    for j in range(PLANE):
        gate_tiles[j] = jnp.concatenate(
            [gate_own[j : j + 1, :], gate_own[PLANE + j : PLANE + j + 1, :], jnp.zeros((6, D), F32)], axis=0
        )
    for a, copy in local:
        if a < 2:
            copy.wait()

    after = plane < PLANES - 1
    pl.semaphore_wait(barrier, len(near) + jnp.where(after, 1 + jnp.where(last, PLANE - 1, 0), 0))

    sent = []

    def remote(src, dst, send_sem, recv_sem, device):
        return pltpu.make_async_remote_copy(
            src_ref=src, dst_ref=dst, send_sem=send_sem, recv_sem=recv_sem, device_id=device, device_id_type=MESH
        )

    def send(*args):
        copy = remote(*args)
        copy.start()
        sent.append(copy)

    def arrived(dst, send_sem, recv_sem):
        remote(dst, dst, send_sem, recv_sem, near[0]).wait_recv()

    def halo_copy(a, j):
        return remote(
            blocks.at[a, j if a % 2 else j // 2, D - 16 : D, :], halo.at[a],
            send_halo.at[a, j], recv_halo.at[a], (plane_at(1) + j, head),
        )

    def raw_send(a):
        for r in range(1, PLANE):
            dest = peer(r)
            send(
                blocks.at[a, dest if a % 2 else dest // 2], raw.at[a, place],
                send_raw.at[a, r - 1], recv_raw.at[a, place], (first + dest, head),
            )
        if a < 3:

            @pl.when(jnp.logical_and(last, after))
            def _():
                for j in range(PLANE):
                    halo_copy(a, j).start()

    raw_send(0)
    for r in range(1, PLANE):
        dest = peer(r)
        send(gate_tiles.at[dest], gates.at[place], send_gate.at[r - 1], recv_gate.at[place], (first + dest, head))
    raw_send(1)
    for a, copy in local:
        if a >= 2:
            copy.wait()

    def raw_arrived(a):
        kept[a].wait()
        for r in range(1, PLANE):
            src = peer(r)
            arrived(raw.at[a, src], send_raw.at[a, 0], recv_raw.at[a, src])
        if a < 3:

            @pl.when(plane > 0)
            def _():
                arrived(halo.at[a], send_halo.at[a, 0], recv_halo.at[a])

    def activate(a):
        ext[a, 0:8, :] = jnp.where(plane > 0, halo[a].astype(F32), 0.0)[8:16]
        for n in range(PLANE):
            ext[a, 8 + n * D : 8 + (n + 1) * D, :] = raw[a, n].astype(F32)
        for n in range(PLANE):
            total = taps[a, 0:1] * ext[a, 5 + n * D : 5 + (n + 1) * D, :]
            for t in range(1, 4):
                total = total + taps[a, t : t + 1] * ext[a, 5 + t + n * D : 5 + t + (n + 1) * D, :]
            total = silu(total)
            if a != 1:
                total = total * lax.rsqrt(jnp.sum(total * total, axis=-1, keepdims=True) + 1e-06)
            if a == 2:
                total = total * D ** (-0.5)
            act[a, n] = total

    gates[place] = gate_tiles[place]
    for r in range(1, PLANE):
        src = peer(r)
        arrived(gates.at[src], send_gate.at[0], recv_gate.at[src])
    chunks = range(PLANE)
    decays = jnp.concatenate([gates[n, 0:1, :] for n in chunks], axis=0)
    rates = jnp.concatenate([gates[n, 1:2, :] for n in chunks], axis=0)
    cum_rows, table = gate_tables(decays, rates)
    row, col = iotas()
    inclusive = row >= col
    cum_col = [jnp.broadcast_to(table[:, n : n + 1], (D, D)) for n in chunks]
    rate_col = [jnp.broadcast_to(table[:, PLANE + n : PLANE + n + 1], (D, D)) for n in chunks]
    within = []
    for n in chunks:
        spread = cum_col[n] - cum_rows[n : n + 1]
        within.append(jnp.where(inclusive, jnp.exp(jnp.where(inclusive, spread, 0.0)), 0.0))
    growth = [jnp.exp(cum_col[n]) for n in chunks]
    tail = [jnp.exp(cum_col[n][D - 1 : D, :] - cum_rows[n : n + 1]) for n in chunks]
    for copy in small[2:]:
        copy.wait()

    raw_arrived(0)

    @pl.when(jnp.logical_and(plane > 0, after))
    def _():
        tell(known.at[0], -1)
        tell(known.at[1], 1)

    raw_send(2)
    activate(0)
    keys = [act[0, n] for n in chunks]
    keys_t = [keys[n].T for n in chunks]
    keys_right = [right(keys_t[n]) for n in chunks]
    key_key = [product(left(keys[n]), keys_right[n]) for n in chunks]
    systems = [jnp.where(row > col, rate_col[n] * within[n] * key_key[n], 0.0) for n in chunks]
    inverse = [left(x) for x in inverses(systems)]
    weighted = [left(keys_t[n] * tail[n]) for n in chunks]
    solved_k = [right(product(inverse[n], right((rate_col[n] * growth[n]) * keys[n]))) for n in chunks]
    maps = []
    for n in chunks:
        m = -product(weighted[n], solved_k[n])
        maps.append((growth[n][D - 1 : D, :], m, left(m)))
    two = [join(maps[n + 1], maps[n]) for n in range(0, PLANE, 2)]
    four = [join(two[n + 1], two[n]) for n in range(0, PLANE // 2, 2)]
    total = join(four[1], four[0])

    row16, _ = iotas(16)

    def put_m(slot, linear):
        d, m, _ = linear
        mine_m[slot, 0:D, :] = m.astype(BF16)
        high, rest = split(d)
        mid, low = split(d - high.astype(F32))
        digits = jnp.where(row16 == 0, high.astype(F32), jnp.where(row16 == 1, mid.astype(F32), low.astype(F32)))
        mine_m[slot, D : D + 16, :] = jnp.where(row16 < 3, digits, 0.0).astype(BF16)

    def m_copy(src, dst, r):
        return remote(mine_m.at[src], got_m.at[dst], send_m.at[dst], recv_m.at[dst], (plane_at(r) + place, head))

    def b_copy(src, dst, r):
        return remote(mine_b.at[src], got_b.at[dst], send_b.at[dst], recv_b.at[dst], (plane_at(r) + place, head))

    hops = {
        "m1": (m_copy(0, 0, 1), 1, 6),
        "m2": (m_copy(1, 1, 2), 2, 5),
        "m4": (m_copy(1, 2, 4), 2, 3),
        "b1": (b_copy(0, 0, 1), 0, 6),
        "b2": (b_copy(1, 1, 2), 0, 5),
        "b4": (b_copy(1, 2, 4), 0, 3),
        "b6": (b_copy(1, 3, 6), 0, 1),
    }

    def hop(name, act_on):
        copy, low, high = hops[name]
        distance = int(name[1])
        shift = 0 if act_on != "wait_recv" else distance

        @pl.when(jnp.logical_and(plane >= low + shift, plane <= high + shift))
        def _():
            getattr(copy, act_on)()

    def take_m(slot, name):
        hop(name, "wait_recv")
        held = jnp.where(plane >= hops[name][1] + int(name[1]), got_m[slot].astype(F32), 0.0)
        return jnp.sum(held[D : D + 16], axis=0, keepdims=True), held[0:D], left(held[0:D])

    def take_b(slot, name):
        hop(name, "wait_recv")
        return jnp.where(plane >= int(name[1]), got_b[slot].astype(F32), 0.0).astype(BF16)

    put_m(0, total)
    hop("m1", "start")

    raw_arrived(1)
    raw_send(3)
    activate(1)
    solved_v = [right(product(inverse[n], right(rate_col[n] * act[1, n]))) for n in chunks]
    offsets = [product(weighted[n], solved_v[n]) for n in chunks]
    two_b = [advance(maps[n + 1], offsets[n + 1], offsets[n]) for n in range(0, PLANE, 2)]
    four_b = [advance(two[n + 1], two_b[n + 1], two_b[n]) for n in range(0, PLANE // 2, 2)]
    total_b = advance(four[1], four_b[1], four_b[0])
    mine_b[0] = total_b.astype(BF16)
    hop("b1", "start")

    @pl.when(plane <= 5)
    def _():
        pl.semaphore_wait(known.at[0], 1)

    @pl.when(plane >= 2)
    def _():
        pl.semaphore_wait(known.at[1], 1)

    @pl.when(jnp.logical_and(plane >= 2, plane <= 5))
    def _():
        tell(known.at[2], -2)

    raw_arrived(2)
    activate(2)
    queries = [act[2, n] for n in chunks]
    scores = [left(within[n] * product(left(queries[n]), keys_right[n])) for n in chunks]
    response = [growth[n] * queries[n] - product(scores[n], solved_k[n]) for n in chunks]
    seen = [product(scores[n], solved_v[n]) for n in chunks]

    one = take_m(0, "m1")
    pair = join(total, one)
    put_m(1, pair)

    @pl.when(plane <= 3)
    def _():
        pl.semaphore_wait(known.at[2], 1)

    @pl.when(jnp.logical_and(plane >= 2, plane <= 3))
    def _():
        tell(known.at[3], -2)

    hop("m4", "start")
    hop("m2", "start")
    one_b = take_b(0, "b1")
    pair_b = product_once(total, one_b) + total_b
    mine_b[1] = pair_b.astype(BF16)
    hop("b4", "start")
    hop("b2", "start")

    @pl.when(plane <= 1)
    def _():
        pl.semaphore_wait(known.at[3], 1)

    hop("b6", "start")

    prefix = {1: maps[0], 2: two[0], 4: four[0]}
    prefix_b = {1: offsets[0], 2: two_b[0], 4: four_b[0]}
    for n, later, later_b, earlier in (
        (3, maps[2], offsets[2], 2),
        (5, maps[4], offsets[4], 4),
        (6, two[2], two_b[2], 4),
        (7, maps[6], offsets[6], 6),
    ):
        prefix[n] = join(later, prefix[earlier])
        prefix_b[n] = advance(later, later_b, prefix_b[earlier])
    reach[0] = left(response[0])
    direct[0] = seen[0]
    for n in range(1, PLANE):
        through = product(
            left(response[n]), jnp.concatenate([right(prefix[n][1]), right(prefix_b[n])], axis=1), 2
        )
        reach[n] = left(through[:, :D] + prefix[n][0] * response[n])
        direct[n] = through[:, D:] + seen[n]
    raw_arrived(3)
    for n in chunks:
        own[n] = silu(raw[3, n].astype(F32)) * gain[...]

    two_back = join(one, take_m(1, "m2"))
    four_back = join(two_back, take_m(2, "m4"))
    state = one_b.astype(F32)
    for linear, slot, name in ((one, 1, "b2"), (two_back, 2, "b4"), (four_back, 3, "b6")):
        state = state + product_once(linear, take_b(slot, name))
    state = right(state)

    lanes = pl.ds(pl.multiple_of(place * D, D), D)
    halves = [slice(h * D // PIECES, (h + 1) * D // PIECES) for h in range(PIECES)]
    for h, rows in enumerate(halves):
        for n in chunks:
            heads_out = product(reach[n, rows, :], state) + direct[n, rows, :]
            scale = lax.rsqrt(jnp.mean(heads_out * heads_out, axis=-1, keepdims=True) + 1e-06)
            back[n, rows, :] = (heads_out * scale * own[n, rows, :]).astype(BF16)
        for r in range(1, PLANE):
            dest = peer(r)
            send(
                back.at[dest, rows, :], whole.at[rows, lanes],
                send_back.at[h, r - 1], recv_back.at[h, place], (first + dest, head),
            )
    whole[:, lanes] = back[place]
    w_copy.wait()

    width = out_ref.shape[1]
    for h, rows in enumerate(halves):
        for r in range(1, PLANE):
            src = peer(r)
            arrived(
                whole.at[rows, pl.ds(pl.multiple_of(src * D, D), D)], send_back.at[h, 0], recv_back.at[h, src]
            )
        for r in (2, 1, 3):
            dest = lax.rem(head + r, HEADS_X)
            weights = w_all[:, pl.ds(pl.multiple_of(dest * width, width), width)]
            x_send[r - 1, rows, :] = jnp.dot(whole[rows, :], weights, preferred_element_type=F32).astype(BF16)
            send(
                x_send.at[r - 1, rows, :], x_got.at[r - 1, rows, :],
                send_x.at[h, r - 1], recv_x.at[h, r - 1], (me, dest),
            )
    weights = w_all[:, pl.ds(pl.multiple_of(head * width, width), width)]
    share = jnp.dot(whole[...], weights, preferred_element_type=F32)
    for h, rows in enumerate(halves):
        part = share[rows]
        for r in (1, 3, 2):
            arrived(x_got.at[r - 1, rows, :], send_x.at[h, r - 1], recv_x.at[h, r - 1])
            part = part + x_got[r - 1, rows, :].astype(F32)
        out_ref[rows, :] = part.astype(BF16)
    for copy in sent:
        copy.wait_send()

    for name in hops:
        hop(name, "wait_send")

    @pl.when(jnp.logical_and(last, after))
    def _():
        for a in range(3):
            for j in range(PLANE):
                halo_copy(a, j).wait_send()


def on_device(q_in, k_in, v_in, z_gate, decay, rate, conv_q, conv_k, conv_v, norm_gain, w_out):
    tok, width = q_in.shape
    dma = pltpu.SemaphoreType.DMA
    return pl.pallas_call(
        kernel,
        out_shape=jax.ShapeDtypeStruct((tok, width), BF16),
        in_specs=[pl.BlockSpec(memory_space=pltpu.HBM)] * 11,
        out_specs=pl.BlockSpec(memory_space=VMEM),
        scratch_shapes=[
            VMEM((4, PLANE, D, D), BF16),
            VMEM((4, PLANE, D, D), BF16),
            VMEM((2 * PLANE, D), F32),
            VMEM((PLANE, 8, D), F32),
            VMEM((PLANE, 8, D), F32),
            VMEM((3, 16, D), BF16),
            VMEM((3, PLANE * D + 8, D), F32),
            VMEM((3, PLANE, D, D), F32),
            VMEM((3, 4, D), F32),
            VMEM((1, D), F32),
            VMEM((PLANE, D, 2 * D), BF16),
            VMEM((PLANE, D, D), F32),
            VMEM((2, D + 16, D), BF16),
            VMEM((3, D + 16, D), BF16),
            VMEM((2, D, D), BF16),
            VMEM((4, D, D), BF16),
            VMEM((PLANE, D, D), F32),
            VMEM((PLANE, D, D), BF16),
            VMEM((tok, PLANE * D), BF16),
            VMEM(w_out.shape, BF16),
            VMEM((HEADS_X - 1, tok, width), BF16),
            VMEM((HEADS_X - 1, tok, width), BF16),
            dma((4, PLANE - 1)), dma((4, PLANE)),
            dma((PLANE - 1,)), dma((PLANE,)),
            dma((3, PLANE)), dma((3,)),
            dma((3,)), dma((3,)),
            dma((4,)), dma((4,)),
            dma((PIECES, PLANE - 1)), dma((PIECES, PLANE)),
            dma((PIECES, HEADS_X - 1)), dma((PIECES, HEADS_X - 1)),
            dma, dma((6,)), dma((4, PLANE)),
            pltpu.SemaphoreType.REGULAR((4,)),
        ],
        compiler_params=pltpu.CompilerParams(
            collective_id=0, has_side_effects=True, vmem_limit_bytes=60 * 1024 * 1024
        ),
    )(q_in, k_in, v_in, z_gate, decay.T, rate.T, conv_q, conv_k, conv_v, norm_gain.reshape(1, D), w_out)


def solution(mesh):
    return jax.shard_map(
        on_device,
        mesh=mesh,
        in_specs=(
            P("seq", "head"),
            P("seq", "head"),
            P("seq", "head"),
            P("seq", "head"),
            P("seq", "head"),
            P("seq", "head"),
            P(None, "head"),
            P(None, "head"),
            P(None, "head"),
            P(),
            P("head", None),
        ),
        out_specs=P("seq", "head"),
        check_vma=False,
    )
```

```python
import jax
import jax.numpy as jnp
from jax import lax
from jax.experimental import pallas as pl
from jax.experimental.pallas import tpu as pltpu
from jax.sharding import PartitionSpec as P

F32 = jnp.float32
BF16 = jnp.bfloat16
D = 128
PLANE = 8
PLANES = 8
HEADS_X = 4
PIECES = 4
MESH = pl.DeviceIdType.MESH
VMEM = pltpu.VMEM


def split(x):
    high = x.astype(BF16)
    return high, (x - high.astype(F32)).astype(BF16)


def left(x):
    high, low = split(x)
    return jnp.concatenate([high, low], axis=1)


def right(x):
    high, low = split(x)
    both = jnp.concatenate([high, low], axis=1)
    return jnp.concatenate([both, both], axis=0)


def product(lhs, rhs, count=1):
    both = jnp.dot(lhs, rhs, preferred_element_type=F32)
    half = both.shape[1] // (2 * count)
    parts = [both[:, 2 * i * half : (2 * i + 1) * half] + both[:, (2 * i + 1) * half : (2 * i + 2) * half] for i in range(count)]
    return parts[0] if count == 1 else jnp.concatenate(parts, axis=1)


def silu(x):
    return x / (1.0 + jnp.exp(-x))


def iotas(rows=D):
    return lax.broadcasted_iota(jnp.int32, (rows, D), 0), lax.broadcasted_iota(jnp.int32, (rows, D), 1)


def gate_tables(decays, rates):
    row, col = iotas()
    upper = (row <= col).astype(BF16)
    high, rest = split(decays)
    mid, low = split(decays - high.astype(F32))
    sums = jnp.dot(jnp.concatenate([high, mid, low], axis=0), upper, preferred_element_type=F32)
    sums = sums[0:PLANE] + sums[PLANE : 2 * PLANE] + sums[2 * PLANE : 3 * PLANE]
    table = jnp.concatenate([sums, rates, jnp.zeros((D - 2 * PLANE, D), F32)], axis=0)
    return sums, table.T


def inverses(systems):
    row, col = iotas()
    count = len(systems)
    diagonal = (row >> 4) == (col >> 4)
    packed = []
    for system in systems:
        blocks = jnp.where(diagonal, system, 0.0)
        rows = blocks[0:16]
        for b in range(1, 8):
            rows = rows + blocks[16 * b : 16 * b + 16]
        packed.append(rows)
    packed = left(jnp.concatenate(packed, axis=0))
    row16, col16 = iotas(16)
    eye = jnp.where(row16 == (col16 & 15), 1.0, 0.0)
    found = jnp.concatenate([eye] * count, axis=0).reshape(count, 16, D)
    same = (row >> 4) == (col >> 4)
    for first in range(0, 15, 2):
        picks = range(first, min(first + 2, 15))
        spread = [(same & ((row & 15) == j)).astype(BF16) for j in picks]
        spread = jnp.concatenate(spread, axis=1)
        spread = jnp.dot(packed, jnp.concatenate([spread, spread], axis=0), preferred_element_type=F32)
        for u, j in enumerate(picks):
            factor = spread[:, u * D : (u + 1) * D].reshape(count, 16, D)
            found = found - factor * found[:, j : j + 1, :]
    result = [jnp.where(diagonal, jnp.concatenate([found[n]] * 8, axis=0), 0.0) for n in range(count)]
    differ = row ^ col
    for level in range(4, 7):
        off = (differ >= (1 << level)) & (differ < (2 << level))
        parts = [left(jnp.where(off, system, 0.0)) for system in systems]
        inner = [product(parts[n], right(result[n])) for n in range(count)]
        result = [result[n] - product(left(result[n]), right(inner[n])) for n in range(count)]
    return result


def product_once(linear, b):
    whole = jnp.dot(linear[2], jnp.concatenate([b, b], axis=0), preferred_element_type=F32)
    return whole + linear[0] * b.astype(F32)


def join(later, earlier):
    d_later, m_later, split_later = later
    d_earlier, m_earlier, _ = earlier
    m = product(split_later, right(m_earlier)) + d_later * m_earlier + d_earlier * m_later
    return d_later * d_earlier, m, left(m)


def advance(later, b_later, b_earlier):
    return product(later[2], right(b_earlier)) + later[0] * b_earlier + b_later


def kernel(
    q_ref, k_ref, v_ref, z_ref, decay_ref, rate_ref, cq_ref, ck_ref, cv_ref, gain_ref, w_ref, out_ref,
    blocks, raw, gate_own, gate_tiles, gates, halo, ext, act, taps, gain, reach, direct,
    mine_m, got_m, mine_b, got_b, own, back, whole, w_all, x_send, x_got,
    send_raw, recv_raw, send_gate, recv_gate, send_halo, recv_halo, send_m, recv_m, send_b, recv_b,
    send_back, recv_back, send_x, recv_x, w_sem, small_sem, block_sem, known,
):
    me, head = lax.axis_index("seq"), lax.axis_index("head")
    plane, place = me // PLANE, lax.rem(me, PLANE)
    first = plane * PLANE
    last = place == PLANE - 1

    def peer(r):
        return lax.rem(place + r, PLANE)

    def plane_at(r):
        return lax.rem(plane + r + PLANES, PLANES) * PLANE

    sources = (k_ref, v_ref, q_ref, z_ref)

    def columns(a, dest):
        return pl.ds(pl.multiple_of((dest if a % 2 else dest // 2) * D, D), D)

    small = [
        pltpu.make_async_copy(src, dst, small_sem.at[i])
        for i, (src, dst) in enumerate(
            [
                (decay_ref, gate_own.at[0:8]),
                (rate_ref, gate_own.at[8:16]),
                (ck_ref.at[:, columns(0, place)], taps.at[0]),
                (cv_ref.at[:, columns(1, place)], taps.at[1]),
                (cq_ref.at[:, columns(2, place)], taps.at[2]),
                (gain_ref, gain),
            ]
        )
    ]
    for copy in small:
        copy.start()

    barrier = pltpu.get_barrier_semaphore()
    near = [(first + peer(r), head) for r in range(1, PLANE)]
    near += [(me, lax.rem(head + r, HEADS_X)) for r in range(1, HEADS_X)]
    for device in near:
        pl.semaphore_signal(barrier, inc=1, device_id=device, device_id_type=MESH)

    def tell(sem, r):
        pl.semaphore_signal(sem, inc=1, device_id=(plane_at(r) + place, head), device_id_type=MESH)

    tell(barrier, -1)

    @pl.when(jnp.logical_and(plane > 0, jnp.logical_not(last)))
    def _():
        pl.semaphore_signal(barrier, inc=1, device_id=(plane_at(-1) + PLANE - 1, head), device_id_type=MESH)

    local = []
    kept = []
    for a in range(4):
        for b in range(PLANE if a % 2 else PLANE // 2):
            copy = pltpu.make_async_copy(
                sources[a].at[:, b * D : (b + 1) * D], blocks.at[a, b], block_sem.at[a, b]
            )
            copy.start()
            local.append((a, copy))
        copy = pltpu.make_async_copy(
            sources[a].at[:, columns(a, place)], raw.at[a, place], recv_raw.at[a, place]
        )
        copy.start()
        kept.append(copy)
    w_copy = pltpu.make_async_copy(w_ref, w_all, w_sem)
    w_copy.start()
    for copy in small[:2]:
        copy.wait()
    for j in range(PLANE):
        gate_tiles[j] = jnp.concatenate(
            [gate_own[j : j + 1, :], gate_own[PLANE + j : PLANE + j + 1, :], jnp.zeros((6, D), F32)], axis=0
        )
    for a, copy in local:
        if a < 2:
            copy.wait()

    after = plane < PLANES - 1
    pl.semaphore_wait(barrier, len(near) + 1 + jnp.where(jnp.logical_and(last, after), PLANE - 1, 0))

    sent = []

    def remote(src, dst, send_sem, recv_sem, device):
        return pltpu.make_async_remote_copy(
            src_ref=src, dst_ref=dst, send_sem=send_sem, recv_sem=recv_sem, device_id=device, device_id_type=MESH
        )

    def send(*args):
        copy = remote(*args)
        copy.start()
        sent.append(copy)

    def arrived(dst, send_sem, recv_sem):
        remote(dst, dst, send_sem, recv_sem, near[0]).wait_recv()

    def halo_copy(a, j):
        return remote(
            blocks.at[a, j if a % 2 else j // 2, D - 16 : D, :], halo.at[a],
            send_halo.at[a, j], recv_halo.at[a], (plane_at(1) + j, head),
        )

    def raw_send(a):
        for r in range(1, PLANE):
            dest = peer(r)
            send(
                blocks.at[a, dest if a % 2 else dest // 2], raw.at[a, place],
                send_raw.at[a, r - 1], recv_raw.at[a, place], (first + dest, head),
            )
        if a < 3:

            @pl.when(jnp.logical_and(last, after))
            def _():
                for j in range(PLANE):
                    halo_copy(a, j).start()

    for r in range(1, PLANE):
        dest = peer(r)
        send(gate_tiles.at[dest], gates.at[place], send_gate.at[r - 1], recv_gate.at[place], (first + dest, head))
    raw_send(0)
    raw_send(1)

    @pl.when(plane == PLANES - 1)
    def _():
        tell(known.at[4], 1)

    for a, copy in local:
        if a >= 2:
            copy.wait()
    raw_send(2)
    raw_send(3)

    def raw_arrived(a):
        kept[a].wait()
        for r in range(1, PLANE):
            src = peer(r)
            arrived(raw.at[a, src], send_raw.at[a, 0], recv_raw.at[a, src])
        if a < 3:

            @pl.when(plane > 0)
            def _():
                arrived(halo.at[a], send_halo.at[a, 0], recv_halo.at[a])

    def activate(a):
        ext[a, 0:8, :] = jnp.where(plane > 0, halo[a].astype(F32), 0.0)[8:16]
        for n in range(PLANE):
            ext[a, 8 + n * D : 8 + (n + 1) * D, :] = raw[a, n].astype(F32)
        for n in range(PLANE):
            total = taps[a, 0:1] * ext[a, 5 + n * D : 5 + (n + 1) * D, :]
            for t in range(1, 4):
                total = total + taps[a, t : t + 1] * ext[a, 5 + t + n * D : 5 + t + (n + 1) * D, :]
            total = silu(total)
            if a != 1:
                total = total * lax.rsqrt(jnp.sum(total * total, axis=-1, keepdims=True) + 1e-06)
            if a == 2:
                total = total * D ** (-0.5)
            act[a, n] = total

    gates[place] = gate_tiles[place]
    for r in range(1, PLANE):
        src = peer(r)
        arrived(gates.at[src], send_gate.at[0], recv_gate.at[src])
    chunks = range(PLANE)
    decays = jnp.concatenate([gates[n, 0:1, :] for n in chunks], axis=0)
    rates = jnp.concatenate([gates[n, 1:2, :] for n in chunks], axis=0)
    cum_rows, table = gate_tables(decays, rates)
    row, col = iotas()
    inclusive = row >= col
    cum_col = [jnp.broadcast_to(table[:, n : n + 1], (D, D)) for n in chunks]
    rate_col = [jnp.broadcast_to(table[:, PLANE + n : PLANE + n + 1], (D, D)) for n in chunks]
    within = []
    for n in chunks:
        spread = cum_col[n] - cum_rows[n : n + 1]
        within.append(jnp.where(inclusive, jnp.exp(jnp.where(inclusive, spread, 0.0)), 0.0))
    growth = [jnp.exp(cum_col[n]) for n in chunks]
    tail = [jnp.exp(cum_col[n][D - 1 : D, :] - cum_rows[n : n + 1]) for n in chunks]
    for copy in small[2:]:
        copy.wait()

    raw_arrived(0)

    @pl.when(jnp.logical_and(plane > 0, after))
    def _():
        tell(known.at[0], -1)
        tell(known.at[1], 1)

    @pl.when(plane == PLANES - 1)
    def _():
        tell(known.at[3], 1)

    @pl.when(plane == 0)
    def _():
        pl.semaphore_wait(known.at[4], 1)
        tell(known.at[3], 1)

    activate(0)
    keys = [act[0, n] for n in chunks]
    keys_t = [keys[n].T for n in chunks]
    keys_right = [right(keys_t[n]) for n in chunks]
    key_key = [product(left(keys[n]), keys_right[n]) for n in chunks]
    systems = [jnp.where(row > col, rate_col[n] * within[n] * key_key[n], 0.0) for n in chunks]
    inverse = [left(x) for x in inverses(systems)]
    weighted = [left(keys_t[n] * tail[n]) for n in chunks]
    @pl.when(plane <= 5)
    def _():
        pl.semaphore_wait(known.at[0], 1)

    @pl.when(plane >= 2)
    def _():
        pl.semaphore_wait(known.at[1], 1)

    @pl.when(jnp.logical_and(plane >= 2, plane <= 5))
    def _():
        tell(known.at[2], -2)

    solved_k = [right(product(inverse[n], right((rate_col[n] * growth[n]) * keys[n]))) for n in chunks]
    maps = []
    for n in chunks:
        m = -product(weighted[n], solved_k[n])
        maps.append((growth[n][D - 1 : D, :], m, left(m)))
    two = [join(maps[n + 1], maps[n]) for n in range(0, PLANE, 2)]
    four = [join(two[n + 1], two[n]) for n in range(0, PLANE // 2, 2)]
    total = join(four[1], four[0])

    row16, _ = iotas(16)

    def put_m(slot, linear):
        d, m, _ = linear
        mine_m[slot, 0:D, :] = m.astype(BF16)
        high, rest = split(d)
        mid, low = split(d - high.astype(F32))
        digits = jnp.where(row16 == 0, high.astype(F32), jnp.where(row16 == 1, mid.astype(F32), low.astype(F32)))
        mine_m[slot, D : D + 16, :] = jnp.where(row16 < 3, digits, 0.0).astype(BF16)

    def m_copy(src, dst, r):
        return remote(mine_m.at[src], got_m.at[dst], send_m.at[dst], recv_m.at[dst], (plane_at(r) + place, head))

    def b_copy(src, dst, r):
        return remote(mine_b.at[src], got_b.at[dst], send_b.at[dst], recv_b.at[dst], (plane_at(r) + place, head))

    hops = {
        "m1": (m_copy(0, 0, 1), 1, 6),
        "m2": (m_copy(1, 1, 2), 2, 5),
        "m4": (m_copy(1, 2, 4), 2, 3),
        "b1": (b_copy(0, 0, 1), 0, 6),
        "b2": (b_copy(1, 1, 2), 0, 5),
        "b4": (b_copy(1, 2, 4), 0, 3),
        "b6": (b_copy(1, 3, 6), 0, 1),
    }

    def hop(name, act_on):
        copy, low, high = hops[name]
        distance = int(name[1])
        shift = 0 if act_on != "wait_recv" else distance

        @pl.when(jnp.logical_and(plane >= low + shift, plane <= high + shift))
        def _():
            getattr(copy, act_on)()

    def take_m(slot, name):
        hop(name, "wait_recv")
        held = jnp.where(plane >= hops[name][1] + int(name[1]), got_m[slot].astype(F32), 0.0)
        return jnp.sum(held[D : D + 16], axis=0, keepdims=True), held[0:D], left(held[0:D])

    def take_b(slot, name):
        hop(name, "wait_recv")
        return jnp.where(plane >= int(name[1]), got_b[slot].astype(F32), 0.0).astype(BF16)

    put_m(0, total)
    hop("m1", "start")

    raw_arrived(1)
    activate(1)
    solved_v = [right(product(inverse[n], right(rate_col[n] * act[1, n]))) for n in chunks]
    offsets = [product(weighted[n], solved_v[n]) for n in chunks]
    two_b = [advance(maps[n + 1], offsets[n + 1], offsets[n]) for n in range(0, PLANE, 2)]
    four_b = [advance(two[n + 1], two_b[n + 1], two_b[n]) for n in range(0, PLANE // 2, 2)]
    total_b = advance(four[1], four_b[1], four_b[0])
    mine_b[0] = total_b.astype(BF16)
    hop("b1", "start")

    raw_arrived(2)
    activate(2)
    queries = [act[2, n] for n in chunks]
    scores = [left(within[n] * product(left(queries[n]), keys_right[n])) for n in chunks]
    response = [growth[n] * queries[n] - product(scores[n], solved_k[n]) for n in chunks]
    seen = [product(scores[n], solved_v[n]) for n in chunks]

    one = take_m(0, "m1")
    pair = join(total, one)
    put_m(1, pair)

    @pl.when(plane <= 3)
    def _():
        pl.semaphore_wait(known.at[2], 1)

    hop("m2", "start")
    hop("m4", "start")
    one_b = take_b(0, "b1")
    pair_b = product_once(total, one_b) + total_b
    mine_b[1] = pair_b.astype(BF16)
    hop("b2", "start")
    hop("b4", "start")

    @pl.when(plane <= 1)
    def _():
        pl.semaphore_wait(known.at[3], 1)

    hop("b6", "start")

    prefix = {1: maps[0], 2: two[0], 4: four[0]}
    prefix_b = {1: offsets[0], 2: two_b[0], 4: four_b[0]}
    for n, later, later_b, earlier in (
        (3, maps[2], offsets[2], 2),
        (5, maps[4], offsets[4], 4),
        (6, two[2], two_b[2], 4),
        (7, maps[6], offsets[6], 6),
    ):
        prefix[n] = join(later, prefix[earlier])
        prefix_b[n] = advance(later, later_b, prefix_b[earlier])
    reach[0] = left(response[0])
    direct[0] = seen[0]
    for n in range(1, PLANE):
        through = product(
            left(response[n]), jnp.concatenate([right(prefix[n][1]), right(prefix_b[n])], axis=1), 2
        )
        reach[n] = left(through[:, :D] + prefix[n][0] * response[n])
        direct[n] = through[:, D:] + seen[n]
    raw_arrived(3)
    for n in chunks:
        own[n] = silu(raw[3, n].astype(F32)) * gain[...]

    two_back = join(one, take_m(1, "m2"))
    four_back = join(two_back, take_m(2, "m4"))
    state = one_b.astype(F32)
    for linear, slot, name in ((one, 1, "b2"), (two_back, 2, "b4"), (four_back, 3, "b6")):
        state = state + product_once(linear, take_b(slot, name))
    state = right(state)

    lanes = pl.ds(pl.multiple_of(place * D, D), D)
    halves = [slice(h * D // PIECES, (h + 1) * D // PIECES) for h in range(PIECES)]
    for h, rows in enumerate(halves):
        heads_out = product(reach[:, rows, :].reshape(-1, 2 * D), state) + direct[:, rows, :].reshape(-1, D)
        scale = lax.rsqrt(jnp.mean(heads_out * heads_out, axis=-1, keepdims=True) + 1e-06)
        gated = heads_out * scale * own[:, rows, :].reshape(-1, D)
        back[:, rows, :] = gated.astype(BF16).reshape(PLANE, -1, D)
        for r in range(1, PLANE):
            dest = peer(r)
            send(
                back.at[dest, rows, :], whole.at[rows, lanes],
                send_back.at[h, r - 1], recv_back.at[h, place], (first + dest, head),
            )
    whole[:, lanes] = back[place]
    w_copy.wait()

    width = out_ref.shape[1]
    for h, rows in enumerate(halves):
        for r in range(1, PLANE):
            src = peer(r)
            arrived(
                whole.at[rows, pl.ds(pl.multiple_of(src * D, D), D)], send_back.at[h, 0], recv_back.at[h, src]
            )
        for r in (2, 1, 3):
            dest = lax.rem(head + r, HEADS_X)
            weights = w_all[:, pl.ds(pl.multiple_of(dest * width, width), width)]
            x_send[r - 1, rows, :] = jnp.dot(whole[rows, :], weights, preferred_element_type=F32).astype(BF16)
            send(
                x_send.at[r - 1, rows, :], x_got.at[r - 1, rows, :],
                send_x.at[h, r - 1], recv_x.at[h, r - 1], (me, dest),
            )
    weights = w_all[:, pl.ds(pl.multiple_of(head * width, width), width)]
    share = jnp.dot(whole[...], weights, preferred_element_type=F32)
    for h, rows in enumerate(halves):
        part = share[rows]
        for r in (1, 3, 2):
            arrived(x_got.at[r - 1, rows, :], send_x.at[h, r - 1], recv_x.at[h, r - 1])
            part = part + x_got[r - 1, rows, :].astype(F32)
        out_ref[rows, :] = part.astype(BF16)
    for copy in sent:
        copy.wait_send()

    for name in hops:
        hop(name, "wait_send")

    @pl.when(jnp.logical_and(last, after))
    def _():
        for a in range(3):
            for j in range(PLANE):
                halo_copy(a, j).wait_send()


def on_device(q_in, k_in, v_in, z_gate, decay, rate, conv_q, conv_k, conv_v, norm_gain, w_out):
    tok, width = q_in.shape
    dma = pltpu.SemaphoreType.DMA
    return pl.pallas_call(
        kernel,
        out_shape=jax.ShapeDtypeStruct((tok, width), BF16),
        in_specs=[pl.BlockSpec(memory_space=pltpu.HBM)] * 11,
        out_specs=pl.BlockSpec(memory_space=VMEM),
        scratch_shapes=[
            VMEM((4, PLANE, D, D), BF16),
            VMEM((4, PLANE, D, D), BF16),
            VMEM((2 * PLANE, D), F32),
            VMEM((PLANE, 8, D), F32),
            VMEM((PLANE, 8, D), F32),
            VMEM((3, 16, D), BF16),
            VMEM((3, PLANE * D + 8, D), F32),
            VMEM((3, PLANE, D, D), F32),
            VMEM((3, 4, D), F32),
            VMEM((1, D), F32),
            VMEM((PLANE, D, 2 * D), BF16),
            VMEM((PLANE, D, D), F32),
            VMEM((2, D + 16, D), BF16),
            VMEM((3, D + 16, D), BF16),
            VMEM((2, D, D), BF16),
            VMEM((4, D, D), BF16),
            VMEM((PLANE, D, D), F32),
            VMEM((PLANE, D, D), BF16),
            VMEM((tok, PLANE * D), BF16),
            VMEM(w_out.shape, BF16),
            VMEM((HEADS_X - 1, tok, width), BF16),
            VMEM((HEADS_X - 1, tok, width), BF16),
            dma((4, PLANE - 1)), dma((4, PLANE)),
            dma((PLANE - 1,)), dma((PLANE,)),
            dma((3, PLANE)), dma((3,)),
            dma((3,)), dma((3,)),
            dma((4,)), dma((4,)),
            dma((PIECES, PLANE - 1)), dma((PIECES, PLANE)),
            dma((PIECES, HEADS_X - 1)), dma((PIECES, HEADS_X - 1)),
            dma, dma((6,)), dma((4, PLANE)),
            pltpu.SemaphoreType.REGULAR((5,)),
        ],
        compiler_params=pltpu.CompilerParams(
            collective_id=0, has_side_effects=True, vmem_limit_bytes=60 * 1024 * 1024
        ),
    )(q_in, k_in, v_in, z_gate, decay.T, rate.T, conv_q, conv_k, conv_v, norm_gain.reshape(1, D), w_out)


def solution(mesh):
    return jax.shard_map(
        on_device,
        mesh=mesh,
        in_specs=(
            P("seq", "head"),
            P("seq", "head"),
            P("seq", "head"),
            P("seq", "head"),
            P("seq", "head"),
            P("seq", "head"),
            P(None, "head"),
            P(None, "head"),
            P(None, "head"),
            P(),
            P("head", None),
        ),
        out_specs=P("seq", "head"),
        check_vma=False,
    )
```

```python
import jax
import jax.numpy as jnp
from jax import lax
from jax.experimental import pallas as pl
from jax.experimental.pallas import tpu as pltpu
from jax.sharding import PartitionSpec as P

F32 = jnp.float32
BF16 = jnp.bfloat16
D = 128
PLANE = 8
PLANES = 8
HEADS_X = 4
PIECES = 4
MESH = pl.DeviceIdType.MESH
VMEM = pltpu.VMEM


def split(x):
    high = x.astype(BF16)
    return high, (x - high.astype(F32)).astype(BF16)


def left(x):
    high, low = split(x)
    return jnp.concatenate([high, low], axis=1)


def right(x):
    high, low = split(x)
    both = jnp.concatenate([high, low], axis=1)
    return jnp.concatenate([both, both], axis=0)


def product(lhs, rhs, count=1):
    both = jnp.dot(lhs, rhs, preferred_element_type=F32)
    half = both.shape[1] // (2 * count)
    parts = [both[:, 2 * i * half : (2 * i + 1) * half] + both[:, (2 * i + 1) * half : (2 * i + 2) * half] for i in range(count)]
    return parts[0] if count == 1 else jnp.concatenate(parts, axis=1)


def silu(x):
    return x / (1.0 + jnp.exp(-x))


def iotas(rows=D):
    return lax.broadcasted_iota(jnp.int32, (rows, D), 0), lax.broadcasted_iota(jnp.int32, (rows, D), 1)


def gate_tables(decays, rates):
    row, col = iotas()
    upper = (row <= col).astype(BF16)
    high, rest = split(decays)
    mid, low = split(decays - high.astype(F32))
    sums = jnp.dot(jnp.concatenate([high, mid, low], axis=0), upper, preferred_element_type=F32)
    sums = sums[0:PLANE] + sums[PLANE : 2 * PLANE] + sums[2 * PLANE : 3 * PLANE]
    table = jnp.concatenate([sums, rates, jnp.zeros((D - 2 * PLANE, D), F32)], axis=0)
    return sums, table.T


def inverses(systems):
    row, col = iotas()
    count = len(systems)
    diagonal = (row >> 4) == (col >> 4)
    packed = []
    for system in systems:
        blocks = jnp.where(diagonal, system, 0.0)
        rows = blocks[0:16]
        for b in range(1, 8):
            rows = rows + blocks[16 * b : 16 * b + 16]
        packed.append(rows)
    packed = left(jnp.concatenate(packed, axis=0))
    row16, col16 = iotas(16)
    eye = jnp.where(row16 == (col16 & 15), 1.0, 0.0)
    found = jnp.concatenate([eye] * count, axis=0).reshape(count, 16, D)
    same = (row >> 4) == (col >> 4)
    for first in range(0, 15, 2):
        picks = range(first, min(first + 2, 15))
        spread = [(same & ((row & 15) == j)).astype(BF16) for j in picks]
        spread = jnp.concatenate(spread, axis=1)
        spread = jnp.dot(packed, jnp.concatenate([spread, spread], axis=0), preferred_element_type=F32)
        for u, j in enumerate(picks):
            factor = spread[:, u * D : (u + 1) * D].reshape(count, 16, D)
            found = found - factor * found[:, j : j + 1, :]
    result = [jnp.where(diagonal, jnp.concatenate([found[n]] * 8, axis=0), 0.0) for n in range(count)]
    differ = row ^ col
    for level in range(4, 7):
        off = (differ >= (1 << level)) & (differ < (2 << level))
        parts = [left(jnp.where(off, system, 0.0)) for system in systems]
        inner = [product(parts[n], right(result[n])) for n in range(count)]
        result = [result[n] - product(left(result[n]), right(inner[n])) for n in range(count)]
    return result


def product_once(linear, b):
    whole = jnp.dot(linear[2], jnp.concatenate([b, b], axis=0), preferred_element_type=F32)
    return whole + linear[0] * b.astype(F32)


def join(later, earlier):
    d_later, m_later, split_later = later
    d_earlier, m_earlier, _ = earlier
    m = product(split_later, right(m_earlier)) + d_later * m_earlier + d_earlier * m_later
    return d_later * d_earlier, m, left(m)


def advance(later, b_later, b_earlier):
    return product(later[2], right(b_earlier)) + later[0] * b_earlier + b_later


def kernel(
    q_ref, k_ref, v_ref, z_ref, decay_ref, rate_ref, cq_ref, ck_ref, cv_ref, gain_ref, w_ref, out_ref,
    blocks, raw, gate_own, gate_tiles, gates, halo, ext, act, taps, gain, reach, direct,
    mine_m, got_m, mine_b, got_b, mid_b, own, back, whole, w_all, x_send, x_got,
    send_raw, recv_raw, send_gate, recv_gate, send_halo, recv_halo, send_m, recv_m, send_b, recv_b,
    send_back, recv_back, send_x, recv_x, w_sem, small_sem, block_sem, known,
):
    me, head = lax.axis_index("seq"), lax.axis_index("head")
    plane, place = me // PLANE, lax.rem(me, PLANE)
    first = plane * PLANE
    last = place == PLANE - 1

    def peer(r):
        return lax.rem(place + r, PLANE)

    def plane_at(r):
        return lax.rem(plane + r + PLANES, PLANES) * PLANE

    sources = (k_ref, v_ref, q_ref, z_ref)

    def columns(a, dest):
        return pl.ds(pl.multiple_of((dest if a % 2 else dest // 2) * D, D), D)

    small = [
        pltpu.make_async_copy(src, dst, small_sem.at[i])
        for i, (src, dst) in enumerate(
            [
                (decay_ref, gate_own.at[0:8]),
                (rate_ref, gate_own.at[8:16]),
                (ck_ref.at[:, columns(0, place)], taps.at[0]),
                (cv_ref.at[:, columns(1, place)], taps.at[1]),
                (cq_ref.at[:, columns(2, place)], taps.at[2]),
                (gain_ref, gain),
            ]
        )
    ]
    for copy in small:
        copy.start()

    barrier = pltpu.get_barrier_semaphore()
    near = [(first + peer(r), head) for r in range(1, PLANE)]
    near += [(me, lax.rem(head + r, HEADS_X)) for r in range(1, HEADS_X)]
    for device in near:
        pl.semaphore_signal(barrier, inc=1, device_id=device, device_id_type=MESH)

    def tell(sem, r):
        pl.semaphore_signal(sem, inc=1, device_id=(plane_at(r) + place, head), device_id_type=MESH)

    @pl.when(plane > 0)
    def _():
        tell(barrier, -1)

    @pl.when(jnp.logical_and(plane > 0, jnp.logical_not(last)))
    def _():
        pl.semaphore_signal(barrier, inc=1, device_id=(plane_at(-1) + PLANE - 1, head), device_id_type=MESH)

    local = []
    kept = []
    for a in range(4):
        for b in range(PLANE if a % 2 else PLANE // 2):
            copy = pltpu.make_async_copy(
                sources[a].at[:, b * D : (b + 1) * D], blocks.at[a, b], block_sem.at[a, b]
            )
            copy.start()
            local.append((a, copy))
        copy = pltpu.make_async_copy(
            sources[a].at[:, columns(a, place)], raw.at[a, place], recv_raw.at[a, place]
        )
        copy.start()
        kept.append(copy)
    w_copy = pltpu.make_async_copy(w_ref, w_all, w_sem)
    w_copy.start()
    for copy in small[:2]:
        copy.wait()
    for j in range(PLANE):
        gate_tiles[j] = jnp.concatenate(
            [gate_own[j : j + 1, :], gate_own[PLANE + j : PLANE + j + 1, :], jnp.zeros((6, D), F32)], axis=0
        )
    for a, copy in local:
        if a < 2:
            copy.wait()

    after = plane < PLANES - 1
    pl.semaphore_wait(barrier, len(near) + jnp.where(after, 1 + jnp.where(last, PLANE - 1, 0), 0))

    sent = []

    def remote(src, dst, send_sem, recv_sem, device):
        return pltpu.make_async_remote_copy(
            src_ref=src, dst_ref=dst, send_sem=send_sem, recv_sem=recv_sem, device_id=device, device_id_type=MESH
        )

    def send(*args):
        copy = remote(*args)
        copy.start()
        sent.append(copy)

    def arrived(dst, send_sem, recv_sem):
        remote(dst, dst, send_sem, recv_sem, near[0]).wait_recv()

    def halo_copy(a, j):
        return remote(
            blocks.at[a, j if a % 2 else j // 2, D - 16 : D, :], halo.at[a],
            send_halo.at[a, j], recv_halo.at[a], (plane_at(1) + j, head),
        )

    def raw_send(a):
        for r in range(1, PLANE):
            dest = peer(r)
            send(
                blocks.at[a, dest if a % 2 else dest // 2], raw.at[a, place],
                send_raw.at[a, r - 1], recv_raw.at[a, place], (first + dest, head),
            )
        if a < 3:

            @pl.when(jnp.logical_and(last, after))
            def _():
                for j in range(PLANE):
                    halo_copy(a, j).start()

    for r in range(1, PLANE):
        dest = peer(r)
        send(gate_tiles.at[dest], gates.at[place], send_gate.at[r - 1], recv_gate.at[place], (first + dest, head))
    raw_send(0)
    raw_send(1)

    for a, copy in local:
        if a >= 2:
            copy.wait()
    raw_send(2)
    raw_send(3)

    def raw_arrived(a):
        kept[a].wait()
        for r in range(1, PLANE):
            src = peer(r)
            arrived(raw.at[a, src], send_raw.at[a, 0], recv_raw.at[a, src])
        if a < 3:

            @pl.when(plane > 0)
            def _():
                arrived(halo.at[a], send_halo.at[a, 0], recv_halo.at[a])

    def activate(a):
        ext[a, 0:8, :] = jnp.where(plane > 0, halo[a].astype(F32), 0.0)[8:16]
        for n in range(PLANE):
            ext[a, 8 + n * D : 8 + (n + 1) * D, :] = raw[a, n].astype(F32)
        for n in range(PLANE):
            total = taps[a, 0:1] * ext[a, 5 + n * D : 5 + (n + 1) * D, :]
            for t in range(1, 4):
                total = total + taps[a, t : t + 1] * ext[a, 5 + t + n * D : 5 + t + (n + 1) * D, :]
            total = silu(total)
            if a != 1:
                total = total * lax.rsqrt(jnp.sum(total * total, axis=-1, keepdims=True) + 1e-06)
            if a == 2:
                total = total * D ** (-0.5)
            act[a, n] = total

    gates[place] = gate_tiles[place]
    for r in range(1, PLANE):
        src = peer(r)
        arrived(gates.at[src], send_gate.at[0], recv_gate.at[src])
    chunks = range(PLANE)
    decays = jnp.concatenate([gates[n, 0:1, :] for n in chunks], axis=0)
    rates = jnp.concatenate([gates[n, 1:2, :] for n in chunks], axis=0)
    cum_rows, table = gate_tables(decays, rates)
    row, col = iotas()
    inclusive = row >= col
    cum_col = [jnp.broadcast_to(table[:, n : n + 1], (D, D)) for n in chunks]
    rate_col = [jnp.broadcast_to(table[:, PLANE + n : PLANE + n + 1], (D, D)) for n in chunks]
    within = []
    for n in chunks:
        spread = cum_col[n] - cum_rows[n : n + 1]
        within.append(jnp.where(inclusive, jnp.exp(jnp.where(inclusive, spread, 0.0)), 0.0))
    growth = [jnp.exp(cum_col[n]) for n in chunks]
    tail = [jnp.exp(cum_col[n][D - 1 : D, :] - cum_rows[n : n + 1]) for n in chunks]
    for copy in small[2:]:
        copy.wait()

    raw_arrived(0)

    @pl.when(jnp.logical_and(plane > 0, after))
    def _():
        tell(known.at[0], -1)
        tell(known.at[1], 1)

    activate(0)
    keys = [act[0, n] for n in chunks]
    keys_t = [keys[n].T for n in chunks]
    keys_right = [right(keys_t[n]) for n in chunks]
    key_key = [product(left(keys[n]), keys_right[n]) for n in chunks]
    systems = [jnp.where(row > col, rate_col[n] * within[n] * key_key[n], 0.0) for n in chunks]
    inverse = [left(x) for x in inverses(systems)]
    weighted = [left(keys_t[n] * tail[n]) for n in chunks]
    @pl.when(plane <= 5)
    def _():
        pl.semaphore_wait(known.at[0], 1)

    @pl.when(plane >= 2)
    def _():
        pl.semaphore_wait(known.at[1], 1)

    @pl.when(jnp.logical_and(plane >= 2, plane <= 5))
    def _():
        tell(known.at[2], -2)

    solved_k = [right(product(inverse[n], right((rate_col[n] * growth[n]) * keys[n]))) for n in chunks]
    maps = []
    for n in chunks:
        m = -product(weighted[n], solved_k[n])
        maps.append((growth[n][D - 1 : D, :], m, left(m)))
    two = [join(maps[n + 1], maps[n]) for n in range(0, PLANE, 2)]
    four = [join(two[n + 1], two[n]) for n in range(0, PLANE // 2, 2)]
    total = join(four[1], four[0])

    row16, _ = iotas(16)

    def put_m(slot, linear):
        d, m, _ = linear
        mine_m[slot, 0:D, :] = m.astype(BF16)
        high, rest = split(d)
        mid, low = split(d - high.astype(F32))
        digits = jnp.where(row16 == 0, high.astype(F32), jnp.where(row16 == 1, mid.astype(F32), low.astype(F32)))
        mine_m[slot, D : D + 16, :] = jnp.where(row16 < 3, digits, 0.0).astype(BF16)

    def m_copy(src, dst, r):
        return remote(mine_m.at[src], got_m.at[dst], send_m.at[dst], recv_m.at[dst], (plane_at(r) + place, head))

    def b_copy(src, dst, r):
        return remote(mine_b.at[src], got_b.at[dst], send_b.at[dst], recv_b.at[dst], (plane_at(r) + place, head))

    hops = {
        "m1": (m_copy(0, 0, 1), 1, 6),
        "m2": (m_copy(1, 1, 2), 2, 5),
        "b1": (b_copy(0, 0, 1), 0, 6),
        "b2": (b_copy(1, 1, 2), 0, 5),
        "b4": (b_copy(2, 2, 4), 0, 3),
    }

    def hop(name, act_on):
        copy, low, high = hops[name]
        distance = int(name[1])
        shift = 0 if act_on != "wait_recv" else distance

        @pl.when(jnp.logical_and(plane >= low + shift, plane <= high + shift))
        def _():
            getattr(copy, act_on)()

    def take_m(slot, name):
        hop(name, "wait_recv")
        held = jnp.where(plane >= hops[name][1] + int(name[1]), got_m[slot].astype(F32), 0.0)
        return jnp.sum(held[D : D + 16], axis=0, keepdims=True), held[0:D], left(held[0:D])

    def take_b(slot, name):
        hop(name, "wait_recv")
        return jnp.where(plane >= int(name[1]), got_b[slot].astype(F32), 0.0).astype(BF16)

    put_m(0, total)
    hop("m1", "start")

    raw_arrived(1)
    activate(1)
    solved_v = [right(product(inverse[n], right(rate_col[n] * act[1, n]))) for n in chunks]
    offsets = [product(weighted[n], solved_v[n]) for n in chunks]
    two_b = [advance(maps[n + 1], offsets[n + 1], offsets[n]) for n in range(0, PLANE, 2)]
    four_b = [advance(two[n + 1], two_b[n + 1], two_b[n]) for n in range(0, PLANE // 2, 2)]
    total_b = advance(four[1], four_b[1], four_b[0])
    mine_b[0] = total_b.astype(BF16)
    hop("b1", "start")

    raw_arrived(2)
    activate(2)
    queries = [act[2, n] for n in chunks]
    scores = [left(within[n] * product(left(queries[n]), keys_right[n])) for n in chunks]
    response = [growth[n] * queries[n] - product(scores[n], solved_k[n]) for n in chunks]
    seen = [product(scores[n], solved_v[n]) for n in chunks]

    one = take_m(0, "m1")
    pair = join(total, one)
    put_m(1, pair)

    @pl.when(plane <= 3)
    def _():
        pl.semaphore_wait(known.at[2], 1)

    hop("m2", "start")
    prefix = {1: maps[0], 2: two[0], 4: four[0]}
    prefix_b = {1: offsets[0], 2: two_b[0], 4: four_b[0]}
    for n, later, later_b, earlier in (
        (3, maps[2], offsets[2], 2),
        (5, maps[4], offsets[4], 4),
        (6, two[2], two_b[2], 4),
        (7, maps[6], offsets[6], 6),
    ):
        prefix[n] = join(later, prefix[earlier])
        prefix_b[n] = advance(later, later_b, prefix_b[earlier])
    reach[0] = left(response[0])
    direct[0] = seen[0]
    for n in range(1, PLANE):
        through = product(
            left(response[n]), jnp.concatenate([right(prefix[n][1]), right(prefix_b[n])], axis=1), 2
        )
        reach[n] = left(through[:, :D] + prefix[n][0] * response[n])
        direct[n] = through[:, D:] + seen[n]
    one_b = take_b(0, "b1")
    pair_b = product_once(total, one_b) + total_b
    mine_b[1] = pair_b.astype(BF16)
    hop("b2", "start")

    mid_b[...] = jnp.zeros_like(mid_b)

    @pl.when(jnp.logical_and(plane >= 2, plane <= 3))
    def _():
        hops["b2"][0].wait_recv()
        mid_b[...] = got_b[1]

    mine_b[2] = (product_once(pair, mid_b[...]) + pair_b).astype(BF16)
    hop("b4", "start")

    raw_arrived(3)
    for n in chunks:
        own[n] = silu(raw[3, n].astype(F32)) * gain[...]

    @pl.when(plane >= 4)
    def _():
        hops["b2"][0].wait_recv()

    two_back = join(one, take_m(1, "m2"))
    state = one_b.astype(F32) + product_once(one, jnp.where(plane >= 2, got_b[1].astype(F32), 0.0).astype(BF16))
    state = state + product_once(two_back, take_b(2, "b4"))
    state = right(state)

    lanes = pl.ds(pl.multiple_of(place * D, D), D)
    halves = [slice(h * D // PIECES, (h + 1) * D // PIECES) for h in range(PIECES)]
    for h, rows in enumerate(halves):
        heads_out = product(reach[:, rows, :].reshape(-1, 2 * D), state) + direct[:, rows, :].reshape(-1, D)
        scale = lax.rsqrt(jnp.mean(heads_out * heads_out, axis=-1, keepdims=True) + 1e-06)
        gated = heads_out * scale * own[:, rows, :].reshape(-1, D)
        back[:, rows, :] = gated.astype(BF16).reshape(PLANE, -1, D)
        for r in range(1, PLANE):
            dest = peer(r)
            send(
                back.at[dest, rows, :], whole.at[rows, lanes],
                send_back.at[h, r - 1], recv_back.at[h, place], (first + dest, head),
            )
    whole[:, lanes] = back[place]
    w_copy.wait()

    width = out_ref.shape[1]
    for h, rows in enumerate(halves):
        for r in range(1, PLANE):
            src = peer(r)
            arrived(
                whole.at[rows, pl.ds(pl.multiple_of(src * D, D), D)], send_back.at[h, 0], recv_back.at[h, src]
            )
        for r in (2, 1, 3):
            dest = lax.rem(head + r, HEADS_X)
            weights = w_all[:, pl.ds(pl.multiple_of(dest * width, width), width)]
            x_send[r - 1, rows, :] = jnp.dot(whole[rows, :], weights, preferred_element_type=F32).astype(BF16)
            send(
                x_send.at[r - 1, rows, :], x_got.at[r - 1, rows, :],
                send_x.at[h, r - 1], recv_x.at[h, r - 1], (me, dest),
            )
    weights = w_all[:, pl.ds(pl.multiple_of(head * width, width), width)]
    share = jnp.dot(whole[...], weights, preferred_element_type=F32)
    for h, rows in enumerate(halves):
        part = share[rows]
        for r in (1, 3, 2):
            arrived(x_got.at[r - 1, rows, :], send_x.at[h, r - 1], recv_x.at[h, r - 1])
            part = part + x_got[r - 1, rows, :].astype(F32)
        out_ref[rows, :] = part.astype(BF16)
    for copy in sent:
        copy.wait_send()

    for name in hops:
        hop(name, "wait_send")

    @pl.when(jnp.logical_and(last, after))
    def _():
        for a in range(3):
            for j in range(PLANE):
                halo_copy(a, j).wait_send()


def on_device(q_in, k_in, v_in, z_gate, decay, rate, conv_q, conv_k, conv_v, norm_gain, w_out):
    tok, width = q_in.shape
    dma = pltpu.SemaphoreType.DMA
    return pl.pallas_call(
        kernel,
        out_shape=jax.ShapeDtypeStruct((tok, width), BF16),
        in_specs=[pl.BlockSpec(memory_space=pltpu.HBM)] * 11,
        out_specs=pl.BlockSpec(memory_space=VMEM),
        scratch_shapes=[
            VMEM((4, PLANE, D, D), BF16),
            VMEM((4, PLANE, D, D), BF16),
            VMEM((2 * PLANE, D), F32),
            VMEM((PLANE, 8, D), F32),
            VMEM((PLANE, 8, D), F32),
            VMEM((3, 16, D), BF16),
            VMEM((3, PLANE * D + 8, D), F32),
            VMEM((3, PLANE, D, D), F32),
            VMEM((3, 4, D), F32),
            VMEM((1, D), F32),
            VMEM((PLANE, D, 2 * D), BF16),
            VMEM((PLANE, D, D), F32),
            VMEM((2, D + 16, D), BF16),
            VMEM((2, D + 16, D), BF16),
            VMEM((3, D, D), BF16),
            VMEM((3, D, D), BF16),
            VMEM((D, D), BF16),
            VMEM((PLANE, D, D), F32),
            VMEM((PLANE, D, D), BF16),
            VMEM((tok, PLANE * D), BF16),
            VMEM(w_out.shape, BF16),
            VMEM((HEADS_X - 1, tok, width), BF16),
            VMEM((HEADS_X - 1, tok, width), BF16),
            dma((4, PLANE - 1)), dma((4, PLANE)),
            dma((PLANE - 1,)), dma((PLANE,)),
            dma((3, PLANE)), dma((3,)),
            dma((2,)), dma((2,)),
            dma((3,)), dma((3,)),
            dma((PIECES, PLANE - 1)), dma((PIECES, PLANE)),
            dma((PIECES, HEADS_X - 1)), dma((PIECES, HEADS_X - 1)),
            dma, dma((6,)), dma((4, PLANE)),
            pltpu.SemaphoreType.REGULAR((3,)),
        ],
        compiler_params=pltpu.CompilerParams(
            collective_id=0, has_side_effects=True, vmem_limit_bytes=60 * 1024 * 1024
        ),
    )(q_in, k_in, v_in, z_gate, decay.T, rate.T, conv_q, conv_k, conv_v, norm_gain.reshape(1, D), w_out)


def solution(mesh):
    return jax.shard_map(
        on_device,
        mesh=mesh,
        in_specs=(
            P("seq", "head"),
            P("seq", "head"),
            P("seq", "head"),
            P("seq", "head"),
            P("seq", "head"),
            P("seq", "head"),
            P(None, "head"),
            P(None, "head"),
            P(None, "head"),
            P(),
            P("head", None),
        ),
        out_specs=P("seq", "head"),
        check_vma=False,
    )
```

```python
import jax
import jax.numpy as jnp
from jax import lax
from jax.experimental import pallas as pl
from jax.experimental.pallas import tpu as pltpu
from jax.sharding import PartitionSpec as P

F32 = jnp.float32
BF16 = jnp.bfloat16
D = 128
PLANE = 8
PLANES = 8
HEADS_X = 4
ROWS = (0, 32, 80, 128)
PIECES = len(ROWS) - 1
MESH = pl.DeviceIdType.MESH
VMEM = pltpu.VMEM


def split(x):
    high = x.astype(BF16)
    return high, (x - high.astype(F32)).astype(BF16)


def left(x):
    high, low = split(x)
    return jnp.concatenate([high, low], axis=1)


def right(x):
    high, low = split(x)
    both = jnp.concatenate([high, low], axis=1)
    return jnp.concatenate([both, both], axis=0)


def product(lhs, rhs, count=1):
    both = jnp.dot(lhs, rhs, preferred_element_type=F32)
    half = both.shape[1] // (2 * count)
    parts = [both[:, 2 * i * half : (2 * i + 1) * half] + both[:, (2 * i + 1) * half : (2 * i + 2) * half] for i in range(count)]
    return parts[0] if count == 1 else jnp.concatenate(parts, axis=1)


def silu(x):
    return x / (1.0 + jnp.exp(-x))


def iotas(rows=D):
    return lax.broadcasted_iota(jnp.int32, (rows, D), 0), lax.broadcasted_iota(jnp.int32, (rows, D), 1)


def gate_tables(decays, rates):
    row, col = iotas()
    upper = (row <= col).astype(BF16)
    high, rest = split(decays)
    mid, low = split(decays - high.astype(F32))
    sums = jnp.dot(jnp.concatenate([high, mid, low], axis=0), upper, preferred_element_type=F32)
    sums = sums[0:PLANE] + sums[PLANE : 2 * PLANE] + sums[2 * PLANE : 3 * PLANE]
    table = jnp.concatenate([sums, rates, jnp.zeros((D - 2 * PLANE, D), F32)], axis=0)
    return sums, table.T


def inverses(systems):
    row, col = iotas()
    count = len(systems)
    diagonal = (row >> 4) == (col >> 4)
    packed = []
    for system in systems:
        blocks = jnp.where(diagonal, system, 0.0)
        rows = blocks[0:16]
        for b in range(1, 8):
            rows = rows + blocks[16 * b : 16 * b + 16]
        packed.append(rows)
    packed = left(jnp.concatenate(packed, axis=0))
    row16, col16 = iotas(16)
    eye = jnp.where(row16 == (col16 & 15), 1.0, 0.0)
    found = jnp.concatenate([eye] * count, axis=0).reshape(count, 16, D)
    same = (row >> 4) == (col >> 4)
    for first in range(0, 15, 2):
        picks = range(first, min(first + 2, 15))
        spread = [(same & ((row & 15) == j)).astype(BF16) for j in picks]
        spread = jnp.concatenate(spread, axis=1)
        spread = jnp.dot(packed, jnp.concatenate([spread, spread], axis=0), preferred_element_type=F32)
        for u, j in enumerate(picks):
            factor = spread[:, u * D : (u + 1) * D].reshape(count, 16, D)
            found = found - factor * found[:, j : j + 1, :]
    result = [jnp.where(diagonal, jnp.concatenate([found[n]] * 8, axis=0), 0.0) for n in range(count)]
    differ = row ^ col
    for level in range(4, 7):
        off = (differ >= (1 << level)) & (differ < (2 << level))
        parts = [left(jnp.where(off, system, 0.0)) for system in systems]
        inner = [product(parts[n], right(result[n])) for n in range(count)]
        result = [result[n] - product(left(result[n]), right(inner[n])) for n in range(count)]
    return result


def product_once(linear, b):
    whole = jnp.dot(linear[2], jnp.concatenate([b, b], axis=0), preferred_element_type=F32)
    return whole + linear[0] * b.astype(F32)


def join(later, earlier):
    d_later, m_later, split_later = later
    d_earlier, m_earlier, _ = earlier
    m = product(split_later, right(m_earlier)) + d_later * m_earlier + d_earlier * m_later
    return d_later * d_earlier, m, left(m)


def advance(later, b_later, b_earlier):
    return product(later[2], right(b_earlier)) + later[0] * b_earlier + b_later


def kernel(
    q_ref, k_ref, v_ref, z_ref, decay_ref, rate_ref, cq_ref, ck_ref, cv_ref, gain_ref, w_ref, out_ref,
    blocks, raw, gate_own, gate_tiles, gates, halo, ext, act, taps, gain, reach, direct,
    mine_m, got_m, mine_b, got_b, mid_b, own, back, whole, w_all, x_send, x_got,
    send_raw, recv_raw, send_gate, recv_gate, send_halo, recv_halo, send_m, recv_m, send_b, recv_b,
    send_back, recv_back, send_x, recv_x, w_sem, small_sem, block_sem, known,
):
    me, head = lax.axis_index("seq"), lax.axis_index("head")
    plane, place = me // PLANE, lax.rem(me, PLANE)
    first = plane * PLANE
    last = place == PLANE - 1

    def peer(r):
        return lax.rem(place + r, PLANE)

    def plane_at(r):
        return lax.rem(plane + r + PLANES, PLANES) * PLANE

    sources = (k_ref, v_ref, q_ref, z_ref)

    def columns(a, dest):
        return pl.ds(pl.multiple_of((dest if a % 2 else dest // 2) * D, D), D)

    barrier = pltpu.get_barrier_semaphore()
    near = [(first + peer(r), head) for r in range(1, PLANE)]
    near += [(me, lax.rem(head + r, HEADS_X)) for r in range(1, HEADS_X)]
    for device in near:
        pl.semaphore_signal(barrier, inc=1, device_id=device, device_id_type=MESH)

    def tell(sem, r):
        pl.semaphore_signal(sem, inc=1, device_id=(plane_at(r) + place, head), device_id_type=MESH)

    @pl.when(plane > 0)
    def _():
        tell(barrier, -1)

    @pl.when(jnp.logical_and(plane > 0, jnp.logical_not(last)))
    def _():
        pl.semaphore_signal(barrier, inc=1, device_id=(plane_at(-1) + PLANE - 1, head), device_id_type=MESH)

    small = [
        pltpu.make_async_copy(src, dst, small_sem.at[i])
        for i, (src, dst) in enumerate(
            [
                (decay_ref, gate_own.at[0:8]),
                (rate_ref, gate_own.at[8:16]),
                (ck_ref.at[:, columns(0, place)], taps.at[0]),
                (cv_ref.at[:, columns(1, place)], taps.at[1]),
                (cq_ref.at[:, columns(2, place)], taps.at[2]),
                (gain_ref, gain),
            ]
        )
    ]
    for copy in small:
        copy.start()

    local = []
    kept = []
    for a in range(4):
        for b in range(PLANE if a % 2 else PLANE // 2):
            copy = pltpu.make_async_copy(
                sources[a].at[:, b * D : (b + 1) * D], blocks.at[a, b], block_sem.at[a, b]
            )
            copy.start()
            local.append((a, copy))
        copy = pltpu.make_async_copy(
            sources[a].at[:, columns(a, place)], raw.at[a, place], recv_raw.at[a, place]
        )
        copy.start()
        kept.append(copy)
    w_copy = pltpu.make_async_copy(w_ref, w_all, w_sem)
    w_copy.start()
    for copy in small[:2]:
        copy.wait()
    for j in range(PLANE):
        gate_tiles[j] = jnp.concatenate(
            [gate_own[j : j + 1, :], gate_own[PLANE + j : PLANE + j + 1, :], jnp.zeros((6, D), F32)], axis=0
        )
    for a, copy in local:
        if a < 2:
            copy.wait()

    after = plane < PLANES - 1
    pl.semaphore_wait(barrier, len(near) + jnp.where(after, 1 + jnp.where(last, PLANE - 1, 0), 0))

    sent = []

    def remote(src, dst, send_sem, recv_sem, device):
        return pltpu.make_async_remote_copy(
            src_ref=src, dst_ref=dst, send_sem=send_sem, recv_sem=recv_sem, device_id=device, device_id_type=MESH
        )

    def send(*args):
        copy = remote(*args)
        copy.start()
        sent.append(copy)

    def arrived(dst, send_sem, recv_sem):
        remote(dst, dst, send_sem, recv_sem, near[0]).wait_recv()

    def halo_copy(a, j):
        return remote(
            blocks.at[a, j if a % 2 else j // 2, D - 16 : D, :], halo.at[a],
            send_halo.at[a, j], recv_halo.at[a], (plane_at(1) + j, head),
        )

    def raw_send(a):
        for r in range(1, PLANE):
            dest = peer(r)
            send(
                blocks.at[a, dest if a % 2 else dest // 2], raw.at[a, place],
                send_raw.at[a, r - 1], recv_raw.at[a, place], (first + dest, head),
            )
        if a < 3:

            @pl.when(jnp.logical_and(last, after))
            def _():
                for j in range(PLANE):
                    halo_copy(a, j).start()

    for r in range(1, PLANE):
        dest = peer(r)
        send(gate_tiles.at[dest], gates.at[place], send_gate.at[r - 1], recv_gate.at[place], (first + dest, head))
    raw_send(0)
    raw_send(1)

    for a, copy in local:
        if a >= 2:
            copy.wait()
    raw_send(2)
    raw_send(3)

    def raw_arrived(a):
        kept[a].wait()
        for r in range(1, PLANE):
            src = peer(r)
            arrived(raw.at[a, src], send_raw.at[a, 0], recv_raw.at[a, src])
        if a < 3:

            @pl.when(plane > 0)
            def _():
                arrived(halo.at[a], send_halo.at[a, 0], recv_halo.at[a])

    def activate(a):
        ext[a, 0:8, :] = jnp.where(plane > 0, halo[a].astype(F32), 0.0)[8:16]
        for n in range(PLANE):
            ext[a, 8 + n * D : 8 + (n + 1) * D, :] = raw[a, n].astype(F32)
        for n in range(PLANE):
            total = taps[a, 0:1] * ext[a, 5 + n * D : 5 + (n + 1) * D, :]
            for t in range(1, 4):
                total = total + taps[a, t : t + 1] * ext[a, 5 + t + n * D : 5 + t + (n + 1) * D, :]
            total = silu(total)
            if a != 1:
                total = total * lax.rsqrt(jnp.sum(total * total, axis=-1, keepdims=True) + 1e-06)
            if a == 2:
                total = total * D ** (-0.5)
            act[a, n] = total

    gates[place] = gate_tiles[place]
    for r in range(1, PLANE):
        src = peer(r)
        arrived(gates.at[src], send_gate.at[0], recv_gate.at[src])
    chunks = range(PLANE)
    decays = jnp.concatenate([gates[n, 0:1, :] for n in chunks], axis=0)
    rates = jnp.concatenate([gates[n, 1:2, :] for n in chunks], axis=0)
    cum_rows, table = gate_tables(decays, rates)
    row, col = iotas()
    inclusive = row >= col
    cum_col = [jnp.broadcast_to(table[:, n : n + 1], (D, D)) for n in chunks]
    rate_col = [jnp.broadcast_to(table[:, PLANE + n : PLANE + n + 1], (D, D)) for n in chunks]
    within = []
    for n in chunks:
        spread = cum_col[n] - cum_rows[n : n + 1]
        within.append(jnp.where(inclusive, jnp.exp(jnp.where(inclusive, spread, 0.0)), 0.0))
    growth = [jnp.exp(cum_col[n]) for n in chunks]
    tail = [jnp.exp(cum_col[n][D - 1 : D, :] - cum_rows[n : n + 1]) for n in chunks]
    for copy in small[2:]:
        copy.wait()

    raw_arrived(0)

    @pl.when(jnp.logical_and(plane > 0, after))
    def _():
        tell(known.at[0], -1)
        tell(known.at[1], 1)

    activate(0)
    keys = [act[0, n] for n in chunks]
    keys_t = [keys[n].T for n in chunks]
    keys_right = [right(keys_t[n]) for n in chunks]
    key_key = [product(left(keys[n]), keys_right[n]) for n in chunks]
    systems = [jnp.where(row > col, rate_col[n] * within[n] * key_key[n], 0.0) for n in chunks]
    inverse = [left(x) for x in inverses(systems)]
    weighted = [left(keys_t[n] * tail[n]) for n in chunks]
    @pl.when(plane <= 5)
    def _():
        pl.semaphore_wait(known.at[0], 1)

    @pl.when(plane >= 2)
    def _():
        pl.semaphore_wait(known.at[1], 1)

    @pl.when(jnp.logical_and(plane >= 2, plane <= 5))
    def _():
        tell(known.at[2], -2)

    solved_k = [right(product(inverse[n], right((rate_col[n] * growth[n]) * keys[n]))) for n in chunks]
    maps = []
    for n in chunks:
        m = -product(weighted[n], solved_k[n])
        maps.append((growth[n][D - 1 : D, :], m, left(m)))
    two = [join(maps[n + 1], maps[n]) for n in range(0, PLANE, 2)]
    four = [join(two[n + 1], two[n]) for n in range(0, PLANE // 2, 2)]
    total = join(four[1], four[0])

    row16, _ = iotas(16)

    def put_m(slot, linear):
        d, m, _ = linear
        mine_m[slot, 0:D, :] = m.astype(BF16)
        high, rest = split(d)
        mid, low = split(d - high.astype(F32))
        digits = jnp.where(row16 == 0, high.astype(F32), jnp.where(row16 == 1, mid.astype(F32), low.astype(F32)))
        mine_m[slot, D : D + 16, :] = jnp.where(row16 < 3, digits, 0.0).astype(BF16)

    def m_copy(src, dst, r):
        return remote(mine_m.at[src], got_m.at[dst], send_m.at[dst], recv_m.at[dst], (plane_at(r) + place, head))

    def b_copy(src, dst, r):
        return remote(mine_b.at[src], got_b.at[dst], send_b.at[dst], recv_b.at[dst], (plane_at(r) + place, head))

    hops = {
        "m1": (m_copy(0, 0, 1), 1, 6),
        "m2": (m_copy(1, 1, 2), 2, 5),
        "b1": (b_copy(0, 0, 1), 0, 6),
        "b2": (b_copy(1, 1, 2), 0, 5),
        "b4": (b_copy(2, 2, 4), 0, 3),
    }

    def hop(name, act_on):
        copy, low, high = hops[name]
        distance = int(name[1])
        shift = 0 if act_on != "wait_recv" else distance

        @pl.when(jnp.logical_and(plane >= low + shift, plane <= high + shift))
        def _():
            getattr(copy, act_on)()

    def take_m(slot, name):
        hop(name, "wait_recv")
        held = jnp.where(plane >= hops[name][1] + int(name[1]), got_m[slot].astype(F32), 0.0)
        return jnp.sum(held[D : D + 16], axis=0, keepdims=True), held[0:D], left(held[0:D])

    def take_b(slot, name):
        hop(name, "wait_recv")
        return jnp.where(plane >= int(name[1]), got_b[slot].astype(F32), 0.0).astype(BF16)

    put_m(0, total)
    hop("m1", "start")

    raw_arrived(1)
    activate(1)
    solved_v = [right(product(inverse[n], right(rate_col[n] * act[1, n]))) for n in chunks]
    offsets = [product(weighted[n], solved_v[n]) for n in chunks]
    two_b = [advance(maps[n + 1], offsets[n + 1], offsets[n]) for n in range(0, PLANE, 2)]
    four_b = [advance(two[n + 1], two_b[n + 1], two_b[n]) for n in range(0, PLANE // 2, 2)]
    total_b = advance(four[1], four_b[1], four_b[0])
    mine_b[0] = total_b.astype(BF16)
    hop("b1", "start")

    raw_arrived(2)
    activate(2)
    queries = [act[2, n] for n in chunks]
    scores = [left(within[n] * product(left(queries[n]), keys_right[n])) for n in chunks]
    response = [growth[n] * queries[n] - product(scores[n], solved_k[n]) for n in chunks]
    seen = [product(scores[n], solved_v[n]) for n in chunks]

    one = take_m(0, "m1")
    pair = join(total, one)
    put_m(1, pair)

    @pl.when(plane <= 3)
    def _():
        pl.semaphore_wait(known.at[2], 1)

    hop("m2", "start")
    prefix = {1: maps[0], 2: two[0], 4: four[0]}
    prefix_b = {1: offsets[0], 2: two_b[0], 4: four_b[0]}
    for n, later, later_b, earlier in (
        (3, maps[2], offsets[2], 2),
        (5, maps[4], offsets[4], 4),
        (6, two[2], two_b[2], 4),
        (7, maps[6], offsets[6], 6),
    ):
        prefix[n] = join(later, prefix[earlier])
        prefix_b[n] = advance(later, later_b, prefix_b[earlier])
    reach[0] = left(response[0])
    direct[0] = seen[0]
    for n in range(1, PLANE):
        through = product(
            left(response[n]), jnp.concatenate([right(prefix[n][1]), right(prefix_b[n])], axis=1), 2
        )
        reach[n] = left(through[:, :D] + prefix[n][0] * response[n])
        direct[n] = through[:, D:] + seen[n]
    one_b = take_b(0, "b1")
    pair_b = product_once(total, one_b) + total_b
    mine_b[1] = pair_b.astype(BF16)
    hop("b2", "start")

    mid_b[...] = jnp.zeros_like(mid_b)

    @pl.when(jnp.logical_and(plane >= 2, plane <= 3))
    def _():
        hops["b2"][0].wait_recv()
        mid_b[...] = got_b[1]

    mine_b[2] = (product_once(pair, mid_b[...]) + pair_b).astype(BF16)
    hop("b4", "start")

    raw_arrived(3)
    for n in chunks:
        own[n] = silu(raw[3, n].astype(F32)) * gain[...]

    @pl.when(plane >= 4)
    def _():
        hops["b2"][0].wait_recv()

    two_back = join(one, take_m(1, "m2"))
    state = one_b.astype(F32) + product_once(one, jnp.where(plane >= 2, got_b[1].astype(F32), 0.0).astype(BF16))
    state = state + product_once(two_back, take_b(2, "b4"))
    state = right(state)

    lanes = pl.ds(pl.multiple_of(place * D, D), D)
    halves = [slice(ROWS[h], ROWS[h + 1]) for h in range(PIECES)]
    for h, rows in enumerate(halves):
        heads_out = product(reach[:, rows, :].reshape(-1, 2 * D), state) + direct[:, rows, :].reshape(-1, D)
        scale = lax.rsqrt(jnp.mean(heads_out * heads_out, axis=-1, keepdims=True) + 1e-06)
        gated = heads_out * scale * own[:, rows, :].reshape(-1, D)
        back[:, rows, :] = gated.astype(BF16).reshape(PLANE, -1, D)
        for r in range(1, PLANE):
            dest = peer(r)
            send(
                back.at[dest, rows, :], whole.at[rows, lanes],
                send_back.at[h, r - 1], recv_back.at[h, place], (first + dest, head),
            )
    whole[:, lanes] = back[place]
    w_copy.wait()

    width = out_ref.shape[1]
    for h, rows in enumerate(halves):
        for r in range(1, PLANE):
            src = peer(r)
            arrived(
                whole.at[rows, pl.ds(pl.multiple_of(src * D, D), D)], send_back.at[h, 0], recv_back.at[h, src]
            )
        for r in (2, 1, 3):
            dest = lax.rem(head + r, HEADS_X)
            weights = w_all[:, pl.ds(pl.multiple_of(dest * width, width), width)]
            x_send[r - 1, rows, :] = jnp.dot(whole[rows, :], weights, preferred_element_type=F32).astype(BF16)
            send(
                x_send.at[r - 1, rows, :], x_got.at[r - 1, rows, :],
                send_x.at[h, r - 1], recv_x.at[h, r - 1], (me, dest),
            )
    weights = w_all[:, pl.ds(pl.multiple_of(head * width, width), width)]
    share = jnp.dot(whole[...], weights, preferred_element_type=F32)
    for h, rows in enumerate(halves):
        part = share[rows]
        for r in (1, 3, 2):
            arrived(x_got.at[r - 1, rows, :], send_x.at[h, r - 1], recv_x.at[h, r - 1])
            part = part + x_got[r - 1, rows, :].astype(F32)
        out_ref[rows, :] = part.astype(BF16)
    for copy in sent:
        copy.wait_send()

    for name in hops:
        hop(name, "wait_send")

    @pl.when(jnp.logical_and(last, after))
    def _():
        for a in range(3):
            for j in range(PLANE):
                halo_copy(a, j).wait_send()


def on_device(q_in, k_in, v_in, z_gate, decay, rate, conv_q, conv_k, conv_v, norm_gain, w_out):
    tok, width = q_in.shape
    dma = pltpu.SemaphoreType.DMA
    return pl.pallas_call(
        kernel,
        out_shape=jax.ShapeDtypeStruct((tok, width), BF16),
        in_specs=[pl.BlockSpec(memory_space=pltpu.HBM)] * 11,
        out_specs=pl.BlockSpec(memory_space=VMEM),
        scratch_shapes=[
            VMEM((4, PLANE, D, D), BF16),
            VMEM((4, PLANE, D, D), BF16),
            VMEM((2 * PLANE, D), F32),
            VMEM((PLANE, 8, D), F32),
            VMEM((PLANE, 8, D), F32),
            VMEM((3, 16, D), BF16),
            VMEM((3, PLANE * D + 8, D), F32),
            VMEM((3, PLANE, D, D), F32),
            VMEM((3, 4, D), F32),
            VMEM((1, D), F32),
            VMEM((PLANE, D, 2 * D), BF16),
            VMEM((PLANE, D, D), F32),
            VMEM((2, D + 16, D), BF16),
            VMEM((2, D + 16, D), BF16),
            VMEM((3, D, D), BF16),
            VMEM((3, D, D), BF16),
            VMEM((D, D), BF16),
            VMEM((PLANE, D, D), F32),
            VMEM((PLANE, D, D), BF16),
            VMEM((tok, PLANE * D), BF16),
            VMEM(w_out.shape, BF16),
            VMEM((HEADS_X - 1, tok, width), BF16),
            VMEM((HEADS_X - 1, tok, width), BF16),
            dma((4, PLANE - 1)), dma((4, PLANE)),
            dma((PLANE - 1,)), dma((PLANE,)),
            dma((3, PLANE)), dma((3,)),
            dma((2,)), dma((2,)),
            dma((3,)), dma((3,)),
            dma((PIECES, PLANE - 1)), dma((PIECES, PLANE)),
            dma((PIECES, HEADS_X - 1)), dma((PIECES, HEADS_X - 1)),
            dma, dma((6,)), dma((4, PLANE)),
            pltpu.SemaphoreType.REGULAR((3,)),
        ],
        compiler_params=pltpu.CompilerParams(
            collective_id=0, has_side_effects=True, vmem_limit_bytes=60 * 1024 * 1024
        ),
    )(q_in, k_in, v_in, z_gate, decay.T, rate.T, conv_q, conv_k, conv_v, norm_gain.reshape(1, D), w_out)


def solution(mesh):
    return jax.shard_map(
        on_device,
        mesh=mesh,
        in_specs=(
            P("seq", "head"),
            P("seq", "head"),
            P("seq", "head"),
            P("seq", "head"),
            P("seq", "head"),
            P("seq", "head"),
            P(None, "head"),
            P(None, "head"),
            P(None, "head"),
            P(),
            P("head", None),
        ),
        out_specs=P("seq", "head"),
        check_vma=False,
    )
```

```python
import jax
import jax.numpy as jnp
from jax import lax
from jax.experimental import pallas as pl
from jax.experimental.pallas import tpu as pltpu
from jax.sharding import PartitionSpec as P

F32 = jnp.float32
BF16 = jnp.bfloat16
D = 128
PLANE = 8
PLANES = 8
HEADS_X = 4
ROWS = (0, 32, 80, 128)
PIECES = len(ROWS) - 1
MESH = pl.DeviceIdType.MESH
VMEM = pltpu.VMEM


def split(x):
    high = x.astype(BF16)
    return high, (x - high.astype(F32)).astype(BF16)


def left(x):
    high, low = split(x)
    return jnp.concatenate([high, low], axis=1)


def right(x):
    high, low = split(x)
    both = jnp.concatenate([high, low], axis=1)
    return jnp.concatenate([both, both], axis=0)


def product(lhs, rhs, count=1):
    both = jnp.dot(lhs, rhs, preferred_element_type=F32)
    half = both.shape[1] // (2 * count)
    parts = [both[:, 2 * i * half : (2 * i + 1) * half] + both[:, (2 * i + 1) * half : (2 * i + 2) * half] for i in range(count)]
    return parts[0] if count == 1 else jnp.concatenate(parts, axis=1)


def silu(x):
    return x / (1.0 + jnp.exp(-x))


def iotas(rows=D):
    return lax.broadcasted_iota(jnp.int32, (rows, D), 0), lax.broadcasted_iota(jnp.int32, (rows, D), 1)


def gate_tables(decays, rates):
    row, col = iotas()
    upper = (row <= col).astype(BF16)
    high, rest = split(decays)
    mid, low = split(decays - high.astype(F32))
    sums = jnp.dot(jnp.concatenate([high, mid, low], axis=0), upper, preferred_element_type=F32)
    sums = sums[0:PLANE] + sums[PLANE : 2 * PLANE] + sums[2 * PLANE : 3 * PLANE]
    table = jnp.concatenate([sums, rates, jnp.zeros((D - 2 * PLANE, D), F32)], axis=0)
    return sums, table.T


def inverses(systems):
    row, col = iotas()
    count = len(systems)
    diagonal = (row >> 4) == (col >> 4)
    packed = []
    for system in systems:
        blocks = jnp.where(diagonal, system, 0.0)
        rows = blocks[0:16]
        for b in range(1, 8):
            rows = rows + blocks[16 * b : 16 * b + 16]
        packed.append(rows)
    packed = left(jnp.concatenate(packed, axis=0))
    row16, col16 = iotas(16)
    eye = jnp.where(row16 == (col16 & 15), 1.0, 0.0)
    found = jnp.concatenate([eye] * count, axis=0).reshape(count, 16, D)
    same = (row >> 4) == (col >> 4)
    for first in range(0, 15, 2):
        picks = range(first, min(first + 2, 15))
        spread = [(same & ((row & 15) == j)).astype(BF16) for j in picks]
        spread = jnp.concatenate(spread, axis=1)
        spread = jnp.dot(packed, jnp.concatenate([spread, spread], axis=0), preferred_element_type=F32)
        for u, j in enumerate(picks):
            factor = spread[:, u * D : (u + 1) * D].reshape(count, 16, D)
            found = found - factor * found[:, j : j + 1, :]
    result = [jnp.where(diagonal, jnp.concatenate([found[n]] * 8, axis=0), 0.0) for n in range(count)]
    differ = row ^ col
    for level in range(4, 7):
        off = (differ >= (1 << level)) & (differ < (2 << level))
        parts = [left(jnp.where(off, system, 0.0)) for system in systems]
        inner = [product(parts[n], right(result[n])) for n in range(count)]
        result = [result[n] - product(left(result[n]), right(inner[n])) for n in range(count)]
    return result


def product_once(linear, b):
    whole = jnp.dot(linear[2], jnp.concatenate([b, b], axis=0), preferred_element_type=F32)
    return whole + linear[0] * b.astype(F32)


def join(later, earlier):
    d_later, m_later, split_later = later
    d_earlier, m_earlier, _ = earlier
    m = product(split_later, right(m_earlier)) + d_later * m_earlier + d_earlier * m_later
    return d_later * d_earlier, m, left(m)


def advance(later, b_later, b_earlier):
    return product(later[2], right(b_earlier)) + later[0] * b_earlier + b_later


def kernel(
    q_ref, k_ref, v_ref, z_ref, decay_ref, rate_ref, cq_ref, ck_ref, cv_ref, gain_ref, w_ref, out_ref,
    blocks, raw, gate_own, gate_tiles, gates, halo, ext, act, taps, gain, reach, direct,
    mine_m, got_m, mine_b, got_b, mid_b, own, back, whole, w_all, x_send, x_got,
    send_raw, recv_raw, send_gate, recv_gate, send_halo, recv_halo, send_m, recv_m, send_b, recv_b,
    send_back, recv_back, send_x, recv_x, w_sem, small_sem, block_sem, known,
):
    me, head = lax.axis_index("seq"), lax.axis_index("head")
    plane, place = me // PLANE, lax.rem(me, PLANE)
    first = plane * PLANE
    last = place == PLANE - 1

    def peer(r):
        return lax.rem(place + r, PLANE)

    def plane_at(r):
        return lax.rem(plane + r + PLANES, PLANES) * PLANE

    sources = (k_ref, v_ref, q_ref, z_ref)

    def columns(a, dest):
        return pl.ds(pl.multiple_of((dest if a % 2 else dest // 2) * D, D), D)

    barrier = pltpu.get_barrier_semaphore()
    near = [(first + peer(r), head) for r in range(1, PLANE)]
    near += [(me, lax.rem(head + r, HEADS_X)) for r in range(1, HEADS_X)]
    for device in near:
        pl.semaphore_signal(barrier, inc=1, device_id=device, device_id_type=MESH)

    def tell(sem, r):
        pl.semaphore_signal(sem, inc=1, device_id=(plane_at(r) + place, head), device_id_type=MESH)

    @pl.when(plane > 0)
    def _():
        tell(barrier, -1)

    @pl.when(jnp.logical_and(plane > 0, jnp.logical_not(last)))
    def _():
        pl.semaphore_signal(barrier, inc=1, device_id=(plane_at(-1) + PLANE - 1, head), device_id_type=MESH)

    small = [
        pltpu.make_async_copy(src, dst, small_sem.at[i])
        for i, (src, dst) in enumerate(
            [
                (decay_ref, gate_own.at[0:8]),
                (rate_ref, gate_own.at[8:16]),
                (ck_ref.at[:, columns(0, place)], taps.at[0]),
                (cv_ref.at[:, columns(1, place)], taps.at[1]),
                (cq_ref.at[:, columns(2, place)], taps.at[2]),
                (gain_ref, gain),
            ]
        )
    ]
    for copy in small:
        copy.start()

    local = []
    kept = []
    for a in range(4):
        for b in range(PLANE if a % 2 else PLANE // 2):
            copy = pltpu.make_async_copy(
                sources[a].at[:, b * D : (b + 1) * D], blocks.at[a, b], block_sem.at[a, b]
            )
            copy.start()
            local.append((a, copy))
        copy = pltpu.make_async_copy(
            sources[a].at[:, columns(a, place)], raw.at[a, place], recv_raw.at[a, place]
        )
        copy.start()
        kept.append(copy)
    w_copy = pltpu.make_async_copy(w_ref, w_all, w_sem)
    w_copy.start()
    for copy in small[:2]:
        copy.wait()
    for j in range(PLANE):
        gate_tiles[j] = jnp.concatenate(
            [gate_own[j : j + 1, :], gate_own[PLANE + j : PLANE + j + 1, :], jnp.zeros((6, D), F32)], axis=0
        )
    for a, copy in local:
        if a < 2:
            copy.wait()

    after = plane < PLANES - 1
    pl.semaphore_wait(barrier, len(near) + jnp.where(after, 1 + jnp.where(last, PLANE - 1, 0), 0))

    sent = []

    def remote(src, dst, send_sem, recv_sem, device):
        return pltpu.make_async_remote_copy(
            src_ref=src, dst_ref=dst, send_sem=send_sem, recv_sem=recv_sem, device_id=device, device_id_type=MESH
        )

    def send(*args):
        copy = remote(*args)
        copy.start()
        sent.append(copy)

    def arrived(dst, send_sem, recv_sem):
        remote(dst, dst, send_sem, recv_sem, near[0]).wait_recv()

    def halo_copy(a, j):
        return remote(
            blocks.at[a, j if a % 2 else j // 2, D - 16 : D, :], halo.at[a],
            send_halo.at[a, j], recv_halo.at[a], (plane_at(1) + j, head),
        )

    def raw_send(a):
        for r in range(1, PLANE):
            dest = peer(r)
            send(
                blocks.at[a, dest if a % 2 else dest // 2], raw.at[a, place],
                send_raw.at[a, r - 1], recv_raw.at[a, place], (first + dest, head),
            )
        if a < 3:

            @pl.when(jnp.logical_and(last, after))
            def _():
                for j in range(PLANE):
                    halo_copy(a, j).start()

    for r in range(1, PLANE):
        dest = peer(r)
        send(gate_tiles.at[dest], gates.at[place], send_gate.at[r - 1], recv_gate.at[place], (first + dest, head))
    raw_send(0)
    raw_send(1)

    for a, copy in local:
        if a >= 2:
            copy.wait()
    raw_send(2)
    raw_send(3)

    def raw_arrived(a):
        kept[a].wait()
        for r in range(1, PLANE):
            src = peer(r)
            arrived(raw.at[a, src], send_raw.at[a, 0], recv_raw.at[a, src])
        if a < 3:

            @pl.when(plane > 0)
            def _():
                arrived(halo.at[a], send_halo.at[a, 0], recv_halo.at[a])

    def activate(a):
        ext[a, 0:8, :] = jnp.where(plane > 0, halo[a].astype(F32), 0.0)[8:16]
        for n in range(PLANE):
            ext[a, 8 + n * D : 8 + (n + 1) * D, :] = raw[a, n].astype(F32)
        for n in range(PLANE):
            total = taps[a, 0:1] * ext[a, 5 + n * D : 5 + (n + 1) * D, :]
            for t in range(1, 4):
                total = total + taps[a, t : t + 1] * ext[a, 5 + t + n * D : 5 + t + (n + 1) * D, :]
            total = silu(total)
            if a != 1:
                total = total * lax.rsqrt(jnp.sum(total * total, axis=-1, keepdims=True) + 1e-06)
            if a == 2:
                total = total * D ** (-0.5)
            act[a, n] = total

    gates[place] = gate_tiles[place]
    for r in range(1, PLANE):
        src = peer(r)
        arrived(gates.at[src], send_gate.at[0], recv_gate.at[src])
    chunks = range(PLANE)
    decays = jnp.concatenate([gates[n, 0:1, :] for n in chunks], axis=0)
    rates = jnp.concatenate([gates[n, 1:2, :] for n in chunks], axis=0)
    cum_rows, table = gate_tables(decays, rates)
    row, col = iotas()
    inclusive = row >= col
    cum_col = [jnp.broadcast_to(table[:, n : n + 1], (D, D)) for n in chunks]
    rate_col = [jnp.broadcast_to(table[:, PLANE + n : PLANE + n + 1], (D, D)) for n in chunks]
    within = []
    for n in chunks:
        spread = cum_col[n] - cum_rows[n : n + 1]
        within.append(jnp.where(inclusive, jnp.exp(jnp.where(inclusive, spread, 0.0)), 0.0))
    growth = [jnp.exp(cum_col[n]) for n in chunks]
    tail = [jnp.exp(cum_col[n][D - 1 : D, :] - cum_rows[n : n + 1]) for n in chunks]
    for copy in small[2:]:
        copy.wait()

    raw_arrived(0)

    @pl.when(jnp.logical_and(plane > 0, after))
    def _():
        tell(known.at[0], -1)
        tell(known.at[1], 1)

    activate(0)
    keys = [act[0, n] for n in chunks]
    keys_t = [keys[n].T for n in chunks]
    keys_right = [right(keys_t[n]) for n in chunks]
    key_key = [product(left(keys[n]), keys_right[n]) for n in chunks]
    systems = [jnp.where(row > col, rate_col[n] * within[n] * key_key[n], 0.0) for n in chunks]
    inverse = [left(x) for x in inverses(systems)]
    weighted = [left(keys_t[n] * tail[n]) for n in chunks]
    @pl.when(plane <= 5)
    def _():
        pl.semaphore_wait(known.at[0], 1)

    @pl.when(plane >= 2)
    def _():
        pl.semaphore_wait(known.at[1], 1)

    @pl.when(jnp.logical_and(plane >= 2, plane <= 5))
    def _():
        tell(known.at[2], -2)

    raw_arrived(1)
    activate(1)
    solved_k = [right(product(inverse[n], right((rate_col[n] * growth[n]) * keys[n]))) for n in chunks]
    maps = []
    for n in chunks:
        m = -product(weighted[n], solved_k[n])
        maps.append((growth[n][D - 1 : D, :], m, left(m)))
    two = [join(maps[n + 1], maps[n]) for n in range(0, PLANE, 2)]
    four = [join(two[n + 1], two[n]) for n in range(0, PLANE // 2, 2)]
    total = join(four[1], four[0])

    row16, _ = iotas(16)

    def put_m(slot, linear):
        d, m, _ = linear
        mine_m[slot, 0:D, :] = m.astype(BF16)
        high, rest = split(d)
        mid, low = split(d - high.astype(F32))
        digits = jnp.where(row16 == 0, high.astype(F32), jnp.where(row16 == 1, mid.astype(F32), low.astype(F32)))
        mine_m[slot, D : D + 16, :] = jnp.where(row16 < 3, digits, 0.0).astype(BF16)

    def m_copy(src, dst, r):
        return remote(mine_m.at[src], got_m.at[dst], send_m.at[dst], recv_m.at[dst], (plane_at(r) + place, head))

    def b_copy(src, dst, r):
        return remote(mine_b.at[src], got_b.at[dst], send_b.at[dst], recv_b.at[dst], (plane_at(r) + place, head))

    hops = {
        "m1": (m_copy(0, 0, 1), 1, 6),
        "m2": (m_copy(1, 1, 2), 2, 5),
        "b1": (b_copy(0, 0, 1), 0, 6),
        "b2": (b_copy(1, 1, 2), 0, 5),
        "b4": (b_copy(2, 2, 4), 0, 3),
    }

    def hop(name, act_on):
        copy, low, high = hops[name]
        distance = int(name[1])
        shift = 0 if act_on != "wait_recv" else distance

        @pl.when(jnp.logical_and(plane >= low + shift, plane <= high + shift))
        def _():
            getattr(copy, act_on)()

    def take_m(slot, name):
        hop(name, "wait_recv")
        held = jnp.where(plane >= hops[name][1] + int(name[1]), got_m[slot].astype(F32), 0.0)
        return jnp.sum(held[D : D + 16], axis=0, keepdims=True), held[0:D], left(held[0:D])

    def take_b(slot, name):
        hop(name, "wait_recv")
        return jnp.where(plane >= int(name[1]), got_b[slot].astype(F32), 0.0).astype(BF16)

    put_m(0, total)
    hop("m1", "start")

    solved_v = [right(product(inverse[n], right(rate_col[n] * act[1, n]))) for n in chunks]
    offsets = [product(weighted[n], solved_v[n]) for n in chunks]
    two_b = [advance(maps[n + 1], offsets[n + 1], offsets[n]) for n in range(0, PLANE, 2)]
    four_b = [advance(two[n + 1], two_b[n + 1], two_b[n]) for n in range(0, PLANE // 2, 2)]
    total_b = advance(four[1], four_b[1], four_b[0])
    mine_b[0] = total_b.astype(BF16)
    hop("b1", "start")

    raw_arrived(2)
    activate(2)
    queries = [act[2, n] for n in chunks]
    scores = [left(within[n] * product(left(queries[n]), keys_right[n])) for n in chunks]
    response = [growth[n] * queries[n] - product(scores[n], solved_k[n]) for n in chunks]
    seen = [product(scores[n], solved_v[n]) for n in chunks]

    one = take_m(0, "m1")
    pair = join(total, one)
    put_m(1, pair)

    @pl.when(plane <= 3)
    def _():
        pl.semaphore_wait(known.at[2], 1)

    hop("m2", "start")
    prefix = {1: maps[0], 2: two[0], 4: four[0]}
    prefix_b = {1: offsets[0], 2: two_b[0], 4: four_b[0]}
    for n, later, later_b, earlier in (
        (3, maps[2], offsets[2], 2),
        (5, maps[4], offsets[4], 4),
        (6, two[2], two_b[2], 4),
        (7, maps[6], offsets[6], 6),
    ):
        prefix[n] = join(later, prefix[earlier])
        prefix_b[n] = advance(later, later_b, prefix_b[earlier])
    reach[0] = left(response[0])
    direct[0] = seen[0]
    for n in range(1, PLANE):
        through = product(
            left(response[n]), jnp.concatenate([right(prefix[n][1]), right(prefix_b[n])], axis=1), 2
        )
        reach[n] = left(through[:, :D] + prefix[n][0] * response[n])
        direct[n] = through[:, D:] + seen[n]
    one_b = take_b(0, "b1")
    pair_b = product_once(total, one_b) + total_b
    mine_b[1] = pair_b.astype(BF16)
    hop("b2", "start")

    mid_b[...] = jnp.zeros_like(mid_b)

    @pl.when(jnp.logical_and(plane >= 2, plane <= 3))
    def _():
        hops["b2"][0].wait_recv()
        mid_b[...] = got_b[1]

    mine_b[2] = (product_once(pair, mid_b[...]) + pair_b).astype(BF16)
    hop("b4", "start")

    raw_arrived(3)
    for n in chunks:
        own[n] = silu(raw[3, n].astype(F32)) * gain[...]

    @pl.when(plane >= 4)
    def _():
        hops["b2"][0].wait_recv()

    two_back = join(one, take_m(1, "m2"))
    state = one_b.astype(F32) + product_once(one, jnp.where(plane >= 2, got_b[1].astype(F32), 0.0).astype(BF16))
    state = state + product_once(two_back, take_b(2, "b4"))
    state = right(state)

    lanes = pl.ds(pl.multiple_of(place * D, D), D)
    halves = [slice(ROWS[h], ROWS[h + 1]) for h in range(PIECES)]
    for h, rows in enumerate(halves):
        heads_out = product(reach[:, rows, :].reshape(-1, 2 * D), state) + direct[:, rows, :].reshape(-1, D)
        scale = lax.rsqrt(jnp.mean(heads_out * heads_out, axis=-1, keepdims=True) + 1e-06)
        gated = heads_out * scale * own[:, rows, :].reshape(-1, D)
        back[:, rows, :] = gated.astype(BF16).reshape(PLANE, -1, D)
        for r in range(1, PLANE):
            dest = peer(r)
            send(
                back.at[dest, rows, :], whole.at[rows, lanes],
                send_back.at[h, r - 1], recv_back.at[h, place], (first + dest, head),
            )
    whole[:, lanes] = back[place]
    w_copy.wait()

    width = out_ref.shape[1]
    for h, rows in enumerate(halves):
        for r in range(1, PLANE):
            src = peer(r)
            arrived(
                whole.at[rows, pl.ds(pl.multiple_of(src * D, D), D)], send_back.at[h, 0], recv_back.at[h, src]
            )
        for r in (2, 1, 3):
            dest = lax.rem(head + r, HEADS_X)
            weights = w_all[:, pl.ds(pl.multiple_of(dest * width, width), width)]
            x_send[r - 1, rows, :] = jnp.dot(whole[rows, :], weights, preferred_element_type=F32).astype(BF16)
            send(
                x_send.at[r - 1, rows, :], x_got.at[r - 1, rows, :],
                send_x.at[h, r - 1], recv_x.at[h, r - 1], (me, dest),
            )
    weights = w_all[:, pl.ds(pl.multiple_of(head * width, width), width)]
    share = jnp.dot(whole[...], weights, preferred_element_type=F32)
    early = len(sent) - PIECES * (HEADS_X - 1)
    for copy in sent[:early]:
        copy.wait_send()

    for name in hops:
        hop(name, "wait_send")

    @pl.when(jnp.logical_and(last, after))
    def _():
        for a in range(3):
            for j in range(PLANE):
                halo_copy(a, j).wait_send()

    for h, rows in enumerate(halves):
        part = share[rows]
        for r in (1, 3, 2):
            arrived(x_got.at[r - 1, rows, :], send_x.at[h, r - 1], recv_x.at[h, r - 1])
            part = part + x_got[r - 1, rows, :].astype(F32)
        out_ref[rows, :] = part.astype(BF16)
    for copy in sent[early:]:
        copy.wait_send()


def on_device(q_in, k_in, v_in, z_gate, decay, rate, conv_q, conv_k, conv_v, norm_gain, w_out):
    tok, width = q_in.shape
    dma = pltpu.SemaphoreType.DMA
    return pl.pallas_call(
        kernel,
        out_shape=jax.ShapeDtypeStruct((tok, width), BF16),
        in_specs=[pl.BlockSpec(memory_space=pltpu.HBM)] * 11,
        out_specs=pl.BlockSpec(memory_space=VMEM),
        scratch_shapes=[
            VMEM((4, PLANE, D, D), BF16),
            VMEM((4, PLANE, D, D), BF16),
            VMEM((2 * PLANE, D), F32),
            VMEM((PLANE, 8, D), F32),
            VMEM((PLANE, 8, D), F32),
            VMEM((3, 16, D), BF16),
            VMEM((3, PLANE * D + 8, D), F32),
            VMEM((3, PLANE, D, D), F32),
            VMEM((3, 4, D), F32),
            VMEM((1, D), F32),
            VMEM((PLANE, D, 2 * D), BF16),
            VMEM((PLANE, D, D), F32),
            VMEM((2, D + 16, D), BF16),
            VMEM((2, D + 16, D), BF16),
            VMEM((3, D, D), BF16),
            VMEM((3, D, D), BF16),
            VMEM((D, D), BF16),
            VMEM((PLANE, D, D), F32),
            VMEM((PLANE, D, D), BF16),
            VMEM((tok, PLANE * D), BF16),
            VMEM(w_out.shape, BF16),
            VMEM((HEADS_X - 1, tok, width), BF16),
            VMEM((HEADS_X - 1, tok, width), BF16),
            dma((4, PLANE - 1)), dma((4, PLANE)),
            dma((PLANE - 1,)), dma((PLANE,)),
            dma((3, PLANE)), dma((3,)),
            dma((2,)), dma((2,)),
            dma((3,)), dma((3,)),
            dma((PIECES, PLANE - 1)), dma((PIECES, PLANE)),
            dma((PIECES, HEADS_X - 1)), dma((PIECES, HEADS_X - 1)),
            dma, dma((6,)), dma((4, PLANE)),
            pltpu.SemaphoreType.REGULAR((3,)),
        ],
        compiler_params=pltpu.CompilerParams(
            collective_id=0, has_side_effects=True, vmem_limit_bytes=60 * 1024 * 1024
        ),
    )(q_in, k_in, v_in, z_gate, decay.T, rate.T, conv_q, conv_k, conv_v, norm_gain.reshape(1, D), w_out)


def solution(mesh):
    return jax.shard_map(
        on_device,
        mesh=mesh,
        in_specs=(
            P("seq", "head"),
            P("seq", "head"),
            P("seq", "head"),
            P("seq", "head"),
            P("seq", "head"),
            P("seq", "head"),
            P(None, "head"),
            P(None, "head"),
            P(None, "head"),
            P(),
            P("head", None),
        ),
        out_specs=P("seq", "head"),
        check_vma=False,
    )
```
